256 devices in a mesh: lat: 32 (over x, z), lon: 8 (over y, core).
Axes of the slice: x: 4, y: 4, z: 8, core: 2. Of those that a mesh axis runs over, the one named last changes fastest.
Arguments:
- prior: float32 [512, 128, 16, 128], P('lat', 'lon'), may hold values from -6 to 6
- stencil_rows: int32 [2, 1024, 4], replicated, may hold values from 0 to 1048560, as said below
- obs_frac: float32 [2, 1024, 2], replicated, may hold values from 0 to 1
- obs_value: float32 [2, 1024], replicated, may hold values from -6 to 6
- obs_var: float32 [2, 1024], replicated, may hold values from 0.25 to 2
Outputs:
- posterior: float32 [512, 128, 16, 128], P('lat', 'lon')
The draws below stay inside these ranges and needn't reach their ends.
Inputs may be any that keep to these rules, and one draw needn't show every extreme that they name: `stencil_rows`: each observation's four rows are the level-0 corners of one grid cell: (a, b), (a + 1, b), (a, b + 1), (a + 1, b + 1) in latitude and longitude, longitude periodic over 128, a at most 510; row = (latitude * 128 + longitude) * 16.
All inputs are finite; a program needn't handle non-finite values.
Results may differ from the reference program's by a relative error of at most 0.0003.
Values sent between devices are 32-bit elements; how exact they have to be, the bound alone decides.
A program may use at most 128 MiB of HBM per device.

```python
import math
import jax
import jax.numpy as jnp
from jax import lax

CLAT = 16
DEPTH = 16
MEMBERS = 128
NOBS = 1024
BATCHES = 2
NLAT = 512
NLON = 128


def draw_stencil_rows(key, part):
    key_lat, key_lon = jax.random.split(jax.random.fold_in(key, 11))
    grid_lat = jax.random.randint(key_lat, (BATCHES, NOBS), 0, NLAT - 1)
    grid_lon = jax.random.randint(key_lon, (BATCHES, NOBS), 0, NLON)
    grid_lat = grid_lat.at[:, 0].set(NLAT - 2).at[:, 1].set(0)
    grid_lon = grid_lon.at[:, 0].set(NLON - 1).at[:, 1].set(0)
    east_lon = (grid_lon + 1) % NLON
    stencil = jnp.stack([(grid_lat * NLON + grid_lon) * DEPTH, ((grid_lat + 1) * NLON + grid_lon) * DEPTH, (grid_lat * NLON + east_lon) * DEPTH, ((grid_lat + 1) * NLON + east_lon) * DEPTH], axis=-1)
    return stencil.astype(jnp.int32)


def level_of(stream_key, shape, cuts, smallest, high):
    def one(axis_at, shards_of):
        steps = jax.random.uniform(jax.random.fold_in(jax.random.fold_in(stream_key, 6), axis_at), (shards_of,), jnp.float32, smallest / len(cuts), high / len(cuts))
        return jnp.repeat(jnp.exp(steps), shape[axis_at] // shards_of).reshape((-1,) + (1,) * (len(shape) - axis_at - 1))

    factor_of = one(*cuts[0])
    for cut in cuts[1:]:
        factor_of = factor_of * one(*cut)
    return factor_of


def bell_draw(rng, shape, scale, limit, pieces=(), dtype=jnp.bfloat16):
    entries = jax.random.normal(rng, shape, jnp.float32) * scale
    if len(pieces) > 0:
        entries = level_of(rng, shape, pieces, -0.22, 0.18) * entries
    return jnp.clip(entries, min=-limit, max=limit).astype(dtype)


def setup_inputs(seed: int = 0) -> dict:
    streams_of = jax.random.split(jax.random.key(seed), 6)
    prior = bell_draw(streams_of[0], (NLAT, NLON, DEPTH, MEMBERS), 1.0, 6.0, ((0, 32), (1, 8)), jnp.float32)
    stencil_rows = draw_stencil_rows(jax.random.fold_in(streams_of[5], 71), 0)
    obs_frac = jnp.clip(jax.random.uniform(streams_of[2], (BATCHES, NOBS, 2), jnp.float32, 0.0, 1.0), 0.0, 1.0)
    obs_value = bell_draw(streams_of[3], (BATCHES, NOBS), 1.0, 6.0, (), jnp.float32)
    obs_var = jnp.clip(jnp.exp(jax.random.uniform(streams_of[4], (BATCHES, NOBS), jnp.float32, math.log(0.25), math.log(2.0))), 0.25, 2.0)
    return dict(prior=prior, stencil_rows=stencil_rows, obs_frac=obs_frac, obs_value=obs_value, obs_var=obs_var)


def taper_gc(distance, radius):
    scaled = distance / radius
    inner_part = (((-0.25 * scaled + 0.5) * scaled + 0.625) * scaled - 5.0 / 3.0) * scaled * scaled + 1.0
    outer_part = ((((scaled / 12.0 - 0.5) * scaled + 0.625) * scaled + 5.0 / 3.0) * scaled - 5.0) * scaled + 4.0 - 2.0 / (3.0 * jnp.maximum(scaled, 1.0))
    return jnp.where(scaled <= 1.0, inner_part, jnp.where(scaled <= 2.0, outer_part, 0.0))

def geometry(stencil, fraction, total_lon, levels):
    corner = stencil[:, 0] // levels
    base_lat = corner // total_lon
    base_lon = corner % total_lon
    frac_lat = fraction[:, 0]
    frac_lon = fraction[:, 1]
    weights = jnp.stack([(1.0 - frac_lat) * (1.0 - frac_lon), frac_lat * (1.0 - frac_lon), (1.0 - frac_lat) * frac_lon, frac_lat * frac_lon], axis=-1)
    obs_lat = base_lat.astype(jnp.float32) + frac_lat
    obs_lon = base_lon.astype(jnp.float32) + frac_lon
    return (weights, obs_lat, obs_lon)

def solve_spread(observed, value, variance, members):
    obs_mean = lax.optimization_barrier(jnp.mean(observed, axis=-1))
    obs_anom = observed - obs_mean[:, None]
    innovation = value - obs_mean
    system = jnp.dot(obs_anom, obs_anom.T, precision=lax.Precision.HIGHEST) / (members - 1.0) + jnp.diag(variance)
    factor = jnp.linalg.cholesky(system)
    mean_part = jax.scipy.linalg.cho_solve((factor, True), innovation)
    anom_part = jax.scipy.linalg.cho_solve((factor, True), obs_anom)
    return mean_part[:, None] - 0.5 * anom_part

def reference(prior, stencil_rows, obs_frac, obs_value, obs_var):
    ensemble = prior
    radius = CLAT * 1.0
    lon_coord = jnp.arange(NLON).astype(jnp.float32)
    for batch_idx in range(BATCHES):
        stencil = stencil_rows[batch_idx]
        weights, obs_lat, obs_lon = geometry(stencil, obs_frac[batch_idx], NLON, DEPTH)
        flat_rows = ensemble.reshape(-1, MEMBERS)
        observed = jnp.zeros((NOBS, MEMBERS), jnp.float32)
        for corner_idx in range(4):
            observed = observed + weights[:, corner_idx, None] * flat_rows[stencil[:, corner_idx]]
        obs_anom = observed - lax.optimization_barrier(jnp.mean(observed, axis=-1, keepdims=True))
        spread = solve_spread(observed, obs_value[batch_idx], obs_var[batch_idx], MEMBERS)
        lon_diff = jnp.abs(lon_coord[:, None] - obs_lon[None, :])
        lon_diff = jnp.minimum(lon_diff, NLON - lon_diff)

        def update_row(packed):
            row_state, lat_value = packed
            lat_diff = lat_value - obs_lat
            distance = jnp.sqrt(lat_diff[None, :] * lat_diff[None, :] + lon_diff * lon_diff)
            taper = taper_gc(distance, radius)
            anomaly = row_state - lax.optimization_barrier(jnp.mean(row_state, axis=-1, keepdims=True))
            covariance = jnp.einsum('ldm,jm->ldj', anomaly, obs_anom, precision=lax.Precision.HIGHEST) / (MEMBERS - 1.0)
            covariance = covariance * taper[:, None, :]
            return row_state + jnp.einsum('ldj,jm->ldm', covariance, spread, precision=lax.Precision.HIGHEST)
        lat_values = jnp.arange(NLAT).astype(jnp.float32)
        ensemble = lax.map(update_row, (ensemble, lat_values))
    return ensemble
```

```python
import functools

import jax
import jax.numpy as jnp
from jax import lax
from jax.experimental import pallas as pl
from jax.experimental.pallas import tpu as pltpu
from jax.sharding import PartitionSpec as P

MESH = pl.DeviceIdType.MESH
F32, BF16 = jnp.float32, jnp.bfloat16
HIGHEST = lax.Precision.HIGHEST
NX, NY, NZ, NC = 4, 4, 8, 2
CL = 16
DEPTH = 16
MEM = 128
NOBS = 1024
NLON = 128
BLK = 128
NB = NOBS // BLK
HB = NB // NC
ROWS = 8
TL = 4


def split(v):
    hi = v.astype(BF16)
    return hi, (v - hi.astype(F32)).astype(BF16)


def split3(v):
    hi = v.astype(BF16)
    rest = v - hi.astype(F32)
    mid = rest.astype(BF16)
    return hi, mid, (rest - mid.astype(F32)).astype(BF16)


def mm(a, b):
    return jnp.dot(a, b, preferred_element_type=F32)


def mm_nt(a, b, precision=None):
    return lax.dot_general(
        a, b, (((1,), (1,)), ((), ())), preferred_element_type=F32, precision=precision
    )


def place():
    lat, lon = lax.axis_index("lat"), lax.axis_index("lon")
    return lat // NZ, lon // NC, lat % NZ, lon % NC


def device(x, y, z, c):
    return (x * NZ + z, y * NC + c)


def observe_kernel(
    bi, ens, st, fr, out, surf, part, got1, acc, got2, local_sem, send, recv
):
    x, y, z, c = place()
    q = x * NY + y
    plane = []
    for r in range(1, NX * NY):
        px, py = lax.rem(x + r // NY, NX), lax.rem(y + r % NY, NY)
        plane.append((px * NY + py, device(px, py, z, c)))
    line = []
    for r in range(1, NZ):
        pz = lax.rem(z + r, NZ)
        line.append((pz, device(x, y, pz, c)))
    other = device(x, y, z, 1 - c)

    def copy(src, dst, stage, target):
        return pltpu.make_async_remote_copy(
            src_ref=src,
            dst_ref=dst,
            send_sem=send.at[stage],
            recv_sem=recv.at[stage],
            device_id=target,
            device_id_type=MESH,
        )

    barrier = pltpu.get_barrier_semaphore()
    partners = [other] + [d for _, d in plane] + [d for _, d in line]
    for target in partners:
        pl.semaphore_signal(barrier, inc=1, device_id=target, device_id_type=MESH)
    own = pltpu.make_async_copy(ens.at[:, :, 0, :], surf.at[c], local_sem)
    own.start()
    pl.semaphore_wait(barrier, len(partners))
    swap = copy(ens.at[:, :, 0, :], surf.at[c], 0, other)
    swap.start()

    span = pl.ds(pl.multiple_of(c * (HB * BLK), BLK), HB * BLK)
    first = st[bi, 0:1, span]
    base_lat = lax.shift_right_logical(first, 11)
    base_lon = lax.shift_right_logical(first, 4) & (NLON - 1)
    east = (base_lon + 1) & (NLON - 1)
    fa, fo = fr[bi, 0:1, span], fr[bi, 1:2, span]
    cells = lax.broadcasted_iota(jnp.int32, (CL, HB * BLK), 0)
    lat = cells + (x * NZ + z) * CL
    w_lat = jnp.where(lat == base_lat, 1.0 - fa, jnp.where(lat == base_lat + 1, fa, 0.0))

    def partial(core):
        lon = cells + (y * NC + core) * CL
        w_lon = jnp.where(lon == base_lon, 1.0 - fo, jnp.where(lon == east, fo, 0.0))
        w = (w_lat[:, None, :] * w_lon[None, :, :]).reshape(CL * CL, HB * BLK)
        s = surf[core].reshape(CL * CL, MEM).T
        s_hi, s_lo = split(s)
        w_hi, w_lo = split(w)
        return mm(s_hi, w_hi) + (mm(s_lo, w_hi) + mm(s_hi, w_lo))

    own.wait()
    mine = partial(c)
    swap.wait_recv()
    total = mine + partial(1 - c)
    for k in range(HB):
        part[k] = total[:, k * BLK : (k + 1) * BLK]

    for r, (pq, target) in enumerate(plane):
        copy(part.at[:, pl.ds(pl.multiple_of(pq * ROWS, ROWS), ROWS), :], got1.at[r], 1, target).start()
    copy(got1, got1, 1, other).wait_recv()
    mine = part[:, pl.ds(pl.multiple_of(q * ROWS, ROWS), ROWS), :]
    for r in range(len(plane)):
        mine = mine + got1[r]
    acc[...] = mine

    half = ROWS * HB // NZ

    def piece(pz):
        return pz // 2, pl.ds(pl.multiple_of((pz % 2) * half, half), half)

    for r, (pz, target) in enumerate(line):
        blk, rows = piece(pz)
        copy(acc.at[blk, rows, :], got2.at[r], 2, target).start()
    copy(got2, got2, 2, other).wait_recv()
    blk, rows = piece(z)
    mine = acc[blk, rows, :]
    for r in range(len(line)):
        mine = mine + got2[r]
    where = (c * HB + blk, pl.ds(pl.multiple_of(q * ROWS + (z % 2) * half, half), half), slice(None))
    out[where] = mine

    for _, target in line:
        copy(out.at[where], out.at[where], 3, target).start()
    copy(got2, got2, 3, other).wait_recv()
    where2 = (pl.ds(c * HB, HB), pl.ds(pl.multiple_of(q * ROWS, ROWS), ROWS), slice(None))
    for _, target in plane:
        copy(out.at[where2], out.at[where2], 4, target).start()
    copy(got1, got1, 4, other).wait_recv()
    last = copy(out.at[pl.ds(c * HB, HB)], out.at[pl.ds(c * HB, HB)], 5, other)
    last.start()
    last.wait_recv()
    swap.wait_send()
    copy(got1, got1, 1, other).wait_send()
    copy(got2, got2, 2, other).wait_send()
    copy(got2, got2, 3, other).wait_send()
    copy(got1, got1, 4, other).wait_send()
    last.wait_send()


def observe(bi, ens, st, fr):
    return pl.pallas_call(
        functools.partial(observe_kernel, bi),
        out_shape=jax.ShapeDtypeStruct((NB, MEM, BLK), F32),
        in_specs=[
            pl.BlockSpec(memory_space=pl.ANY),
            pl.BlockSpec(memory_space=pltpu.VMEM),
            pl.BlockSpec(memory_space=pltpu.VMEM),
        ],
        out_specs=pl.BlockSpec(memory_space=pltpu.VMEM),
        scratch_shapes=[
            pltpu.VMEM((NC, CL, CL, MEM), F32),
            pltpu.VMEM((HB, MEM, BLK), F32),
            pltpu.VMEM((NX * NY - 1, HB, ROWS, BLK), F32),
            pltpu.VMEM((HB, ROWS, BLK), F32),
            pltpu.VMEM((NZ - 1, ROWS * HB // NZ, BLK), F32),
            pltpu.SemaphoreType.DMA,
            pltpu.SemaphoreType.DMA((6,)),
            pltpu.SemaphoreType.DMA((6,)),
        ],
        compiler_params=pltpu.CompilerParams(
            collective_id=bi, has_side_effects=True, vmem_limit_bytes=32 << 20
        ),
        name="observe",
    )(ens, st, fr)


def inverse(m):
    n = m.shape[0]
    row_id = lax.broadcasted_iota(jnp.int32, (n, n), 0)
    col_id = lax.broadcasted_iota(jnp.int32, (n, n), 1)
    for k in range(n):
        inv = 1.0 / m[k : k + 1, k : k + 1]
        row = m[k : k + 1, :] * inv
        col = m[:, k : k + 1]
        swept = m - col * row
        swept = jnp.where(col_id == k, col * inv, swept)
        m = jnp.where(row_id == k, jnp.where(col_id == k, -inv, row), swept)
    return -m


def taper_gc(scaled):
    inner_part = (
        ((-0.25 * scaled + 0.5) * scaled + 0.625) * scaled - 5.0 / 3.0
    ) * scaled * scaled + 1.0
    outer_part = (
        ((((scaled / 12.0 - 0.5) * scaled + 0.625) * scaled + 5.0 / 3.0) * scaled - 5.0) * scaled
        + 4.0
        - 2.0 / (3.0 * jnp.maximum(scaled, 1.0))
    )
    return jnp.where(scaled <= 1.0, inner_part, jnp.where(scaled <= 2.0, outer_part, 0.0))


META = 16


def update_kernel(
    bi, ens, observed, st, fr, value, variance, out, anom, packed, chosen, apack, spack, meta
):
    x, y, z, c = place()
    lat0 = ((x * NZ + z) * CL).astype(F32)
    lon0 = ((y * NC + c) * CL).astype(F32)

    var_row = variance[bi : bi + 1, :]
    inv_row = 1.0 / var_row
    for k in range(NB):
        lanes = slice(k * BLK, (k + 1) * BLK)
        block = observed[k]
        mean = jnp.sum(block, axis=0, keepdims=True) / MEM
        block = block - mean
        anom[0:MEM, lanes] = block
        anom[MEM : MEM + 8, lanes] = jnp.broadcast_to(value[bi : bi + 1, lanes] - mean, (8, BLK))
        hi, lo = split(block)
        packed[0:MEM, lanes] = hi
        packed[MEM : 2 * MEM, lanes] = lo
    innovation = anom[MEM : MEM + 1, :]
    gram = mm_nt(anom[0:MEM, :] * inv_row, anom[...], HIGHEST)
    eye = (
        lax.broadcasted_iota(jnp.int32, (MEM, MEM), 0)
        == lax.broadcasted_iota(jnp.int32, (MEM, MEM), 1)
    )
    inv = inverse(gram[:, 0:MEM] + jnp.where(eye, MEM - 1.0, 0.0))
    h = jnp.sum(inv * gram[:, MEM : MEM + 1], axis=0, keepdims=True)
    factor = (0.5 * (MEM - 1.0)) * inv + h

    first = st[bi, 0:1, :]
    obs_lat = lax.shift_right_logical(first, 11).astype(F32) + fr[bi, 0:1, :]
    obs_lon = (lax.shift_right_logical(first, 4) & (NLON - 1)).astype(F32) + fr[bi, 1:2, :]
    half = 0.5 * (CL - 1)
    d_lat = jnp.maximum(jnp.abs(obs_lat - (lat0 + half)) - half, 0.0)
    d_lon = jnp.abs(obs_lon - (lon0 + half))
    d_lon = jnp.maximum(jnp.minimum(d_lon, NLON - d_lon) - half, 0.0)
    reach = 2.0 * CL
    near = jnp.where(d_lat * d_lat + d_lon * d_lon <= reach * reach + 0.5, 1.0, 0.0)
    rows = jnp.concatenate([near[:, k * BLK : (k + 1) * BLK] for k in range(NB)], axis=0)
    before = (
        lax.broadcasted_iota(jnp.int32, (BLK, BLK), 0)
        < lax.broadcasted_iota(jnp.int32, (BLK, BLK), 1)
    )
    rank = mm(rows.astype(BF16), jnp.where(before, 1.0, 0.0).astype(BF16))
    count = mm(rows.astype(BF16), jnp.ones((BLK, BLK), BF16))
    offset = jnp.zeros((1, BLK), F32)
    for k in range(NB):
        chosen[k : k + 1, :] = jnp.where(
            rows[k : k + 1, :] > 0.0, rank[k : k + 1, :] + offset, -1.0
        )
        offset = offset + count[k : k + 1, :]
    chunks = (jnp.sum(near).astype(jnp.int32) + (BLK - 1)) // BLK

    zero = jnp.zeros((1, NOBS), BF16)
    lines = [*split3(obs_lat), *split3(obs_lon), *split3(inv_row), *split3(innovation)]
    packed[2 * MEM :, :] = jnp.concatenate(lines + [zero] * (META - len(lines)), axis=0)

    def gather(chunk, carry):
        slot = lax.broadcasted_iota(jnp.int32, (BLK, BLK), 0).astype(F32) + (chunk * BLK).astype(F32)
        pick = jnp.concatenate(
            [jnp.where(chosen[k : k + 1, :] == slot, 1.0, 0.0).astype(BF16) for k in range(NB)],
            axis=1,
        )
        got = mm_nt(packed[...], pick)
        near_anom = got[0:MEM] + got[MEM : 2 * MEM]

        def line(k):
            r = 2 * MEM + 3 * k
            return got[r : r + 1] + (got[r + 1 : r + 2] + got[r + 2 : r + 3])

        near_spread = (
            line(3) - jnp.dot(factor, near_anom, preferred_element_type=F32, precision=HIGHEST)
        ).T
        for ref, val in ((apack, near_anom), (spack, near_spread)):
            both = jnp.concatenate(split(val), axis=1)
            ref[chunk, 0:MEM, :] = both
            ref[chunk, MEM:, :] = both
        meta[chunk, 0:1, :] = line(0)
        meta[chunk, 1:2, :] = line(1)
        meta[chunk, 2:3, :] = line(2) / (MEM - 1.0)
        return carry

    lax.fori_loop(0, chunks, gather, 0)

    def rows_of(step, carry):
        lats = pl.ds(step * TL, TL)
        state = ens[lats]
        anomaly = state - jnp.mean(state, axis=-1, keepdims=True)
        left = jnp.concatenate(split(anomaly.reshape(TL * CL * DEPTH, MEM)), axis=1)
        out[lats] = state

        def add(chunk, carry):
            lon = lax.broadcasted_iota(jnp.int32, (CL, BLK), 0).astype(F32) + lon0
            lon_diff = jnp.abs(lon - meta[chunk, 1:2, :])
            lon_diff = jnp.minimum(lon_diff, NLON - lon_diff)
            tapers = []
            for i in range(TL):
                lat_diff = (lat0 + (step * TL + i).astype(F32)) - meta[chunk, 0:1, :]
                distance = jnp.sqrt(lat_diff * lat_diff + lon_diff * lon_diff)
                tapers.append(taper_gc(distance / CL) * meta[chunk, 2:3, :])
            taper = jnp.stack(tapers)
            cov = mm(left, apack[chunk])
            cov = (cov[:, 0:BLK] + cov[:, BLK:]).reshape(TL, CL, DEPTH, BLK) * taper[:, :, None, :]
            cov = jnp.concatenate(split(cov.reshape(TL * CL * DEPTH, BLK)), axis=1)
            delta = mm(cov, spack[chunk])
            delta = delta[:, 0:MEM] + delta[:, MEM:]
            out[lats] = out[lats] + delta.reshape(TL, CL, DEPTH, MEM)
            return carry

        return lax.fori_loop(0, chunks, add, carry)

    lax.fori_loop(0, CL // TL, rows_of, 0)


def update(bi, ens, observed, st, fr, value, variance):
    vmem = pl.BlockSpec(memory_space=pltpu.VMEM)
    return pl.pallas_call(
        functools.partial(update_kernel, bi),
        out_shape=jax.ShapeDtypeStruct(ens.shape, F32),
        in_specs=[vmem] * 6,
        out_specs=vmem,
        scratch_shapes=[
            pltpu.VMEM((MEM + 8, NOBS), F32),
            pltpu.VMEM((2 * MEM + META, NOBS), BF16),
            pltpu.VMEM((NB, BLK), F32),
            pltpu.VMEM((NB, 2 * MEM, 2 * BLK), BF16),
            pltpu.VMEM((NB, 2 * BLK, 2 * MEM), BF16),
            pltpu.VMEM((NB, 8, BLK), F32),
        ],
        compiler_params=pltpu.CompilerParams(vmem_limit_bytes=48 << 20),
        name="update",
    )(ens, observed, st, fr, value, variance)


def local(prior, stencil_rows, obs_frac, obs_value, obs_var):
    st = jnp.transpose(stencil_rows, (0, 2, 1))
    fr = jnp.transpose(obs_frac, (0, 2, 1))
    ens = prior
    for bi in range(stencil_rows.shape[0]):
        observed = observe(bi, ens, st, fr)
        ens = update(bi, ens, observed, st, fr, obs_value, obs_var)
    return ens


def solution(mesh):
    placed = (P("lat", "lon", None, None), P(), P(), P(), P())
    return jax.shard_map(
        local, mesh=mesh, in_specs=placed, out_specs=P("lat", "lon", None, None), check_vma=False
    )
```

```python
import functools

import jax
import jax.numpy as jnp
from jax import lax
from jax.experimental import pallas as pl
from jax.experimental.pallas import tpu as pltpu
from jax.sharding import PartitionSpec as P

MESH = pl.DeviceIdType.MESH
F32, BF16 = jnp.float32, jnp.bfloat16
HIGHEST = lax.Precision.HIGHEST
NX, NY, NZ, NC = 4, 4, 8, 2
CL = 16
DEPTH = 16
MEM = 128
NOBS = 1024
NLON = 128
BLK = 128
NB = NOBS // BLK
HB = NB // NC
ROWS = 8
TL = 4
STEPS = 13


def split(v):
    hi = v.astype(BF16)
    return hi, (v - hi.astype(F32)).astype(BF16)


def split3(v):
    hi = v.astype(BF16)
    rest = v - hi.astype(F32)
    mid = rest.astype(BF16)
    return hi, mid, (rest - mid.astype(F32)).astype(BF16)


def mm(a, b):
    return jnp.dot(a, b, preferred_element_type=F32)


def mm_nt(a, b, precision=None):
    return lax.dot_general(
        a, b, (((1,), (1,)), ((), ())), preferred_element_type=F32, precision=precision
    )


def place():
    lat, lon = lax.axis_index("lat"), lax.axis_index("lon")
    return lat // NZ, lon // NC, lat % NZ, lon % NC


def device(x, y, z, c):
    return (x * NZ + z, y * NC + c)


def eye(scale):
    diagonal = lax.broadcasted_iota(jnp.int32, (MEM, MEM), 0) == lax.broadcasted_iota(
        jnp.int32, (MEM, MEM), 1
    )
    return jnp.where(diagonal, scale, 0.0)


def dot(a, b):
    return jnp.dot(a, b, preferred_element_type=F32, precision=HIGHEST)


def inverse_start(m):
    bound = jnp.max(jnp.sum(jnp.abs(m), axis=0, keepdims=True), axis=1, keepdims=True)
    scale = 1.0 / bound
    return jnp.concatenate([eye(1.0) * scale, m * scale], axis=0), (MEM - 1.0) * scale


def inverse_step(xy, low):
    s = jnp.minimum(2.0 / (1.0 + low), 1.95)
    z = eye(2.0) * s - xy[MEM:, :] * (s * s)
    t = s * low
    return dot(xy, z), jnp.minimum(t * (2.0 - t), s * (2.0 - s))


def inverse_finish(m, x):
    return x + dot(x, eye(1.0) - dot(m, x))


def taper_gc(scaled):
    inner_part = (
        ((-0.25 * scaled + 0.5) * scaled + 0.625) * scaled - 5.0 / 3.0
    ) * scaled * scaled + 1.0
    outer_part = (
        ((((scaled / 12.0 - 0.5) * scaled + 0.625) * scaled + 5.0 / 3.0) * scaled - 5.0) * scaled
        + 4.0
        - 2.0 / (3.0 * jnp.maximum(scaled, 1.0))
    )
    return jnp.where(scaled <= 1.0, inner_part, jnp.where(scaled <= 2.0, outer_part, 0.0))


def positions(st, fr, bi, lanes):
    first = st[bi, 0:1, lanes]
    obs_lat = lax.shift_right_logical(first, 11).astype(F32) + fr[bi, 0:1, lanes]
    obs_lon = (lax.shift_right_logical(first, 4) & (NLON - 1)).astype(F32) + fr[bi, 1:2, lanes]
    return obs_lat, obs_lon


def centre(observed, value, bi, anom, packed):
    for k in range(NB):
        lanes = slice(k * BLK, (k + 1) * BLK)
        block = observed[k]
        mean = jnp.sum(block, axis=0, keepdims=True) / MEM
        block = block - mean
        anom[0:MEM, lanes] = block
        anom[MEM : MEM + 8, lanes] = jnp.broadcast_to(value[bi : bi + 1, lanes] - mean, (8, BLK))
        hi, lo = split(block)
        packed[0:MEM, lanes] = hi
        packed[MEM : 2 * MEM, lanes] = lo


def normal(anom, inv_row):
    gram = mm_nt(anom[0:MEM, :] * inv_row, anom[...], HIGHEST)
    return gram[:, 0:MEM] + eye(MEM - 1.0), gram[:, MEM : MEM + 1]


def spread_factor(inv, g):
    return (0.5 * (MEM - 1.0)) * inv + jnp.sum(inv * g, axis=0, keepdims=True)


def observe_kernel(
    ens, st_in, fr_in, value_in, var_in, out0, out1, factor_out,
    st, fr, value, variance, surf, part, got1, got2, anom, packed, taper, load, send, recv,
):
    x, y, z, c = place()
    q = x * NY + y
    plane = []
    for r in range(1, NX * NY):
        px, py = lax.rem(x + r // NY, NX), lax.rem(y + r % NY, NY)
        plane.append((px * NY + py, device(px, py, z, c)))
    line = [device(x, y, lax.rem(z + r, NZ), c) for r in range(1, NZ)]
    other = device(x, y, z, 1 - c)

    def copy(src, dst, bi, stage, target):
        return pltpu.make_async_remote_copy(
            src_ref=src,
            dst_ref=dst,
            send_sem=send.at[bi, stage],
            recv_sem=recv.at[bi, stage],
            device_id=target,
            device_id_type=MESH,
        )

    loads = [
        pltpu.make_async_copy(ens.at[:, :, 0, :], surf.at[0, c], load.at[0]),
        pltpu.make_async_copy(st_in, st, load.at[1]),
        pltpu.make_async_copy(fr_in, fr, load.at[2]),
        pltpu.make_async_copy(value_in, value, load.at[3]),
        pltpu.make_async_copy(var_in, variance, load.at[4]),
    ]
    for one in loads:
        one.start()
    barrier = pltpu.get_barrier_semaphore()
    partners = [other] + [d for _, d in plane] + line
    for target in partners:
        pl.semaphore_signal(barrier, inc=1, device_id=target, device_id_type=MESH)
    for one in loads:
        one.wait()

    span = pl.ds(pl.multiple_of(c * (HB * BLK), BLK), HB * BLK)
    cells = lax.broadcasted_iota(jnp.int32, (CL, HB * BLK), 0)
    members = pl.ds(pl.multiple_of(q * ROWS, ROWS), ROWS)
    blocks = pl.ds(c * HB, HB)

    def partial(bi, core):
        first = st[bi, 0:1, span]
        base_lat = lax.shift_right_logical(first, 11)
        base_lon = lax.shift_right_logical(first, 4) & (NLON - 1)
        east = (base_lon + 1) & (NLON - 1)
        fa, fo = fr[bi, 0:1, span], fr[bi, 1:2, span]
        lat = cells + (x * NZ + z) * CL
        lon = cells + (y * NC + core) * CL
        w_lat = jnp.where(lat == base_lat, 1.0 - fa, jnp.where(lat == base_lat + 1, fa, 0.0))
        w_lon = jnp.where(lon == base_lon, 1.0 - fo, jnp.where(lon == east, fo, 0.0))
        w = (w_lat[:, None, :] * w_lon[None, :, :]).reshape(CL * CL, HB * BLK)
        s_hi, s_lo = split(surf[bi, core].reshape(CL * CL, MEM).T)
        w_hi, w_lo = split(w)
        return mm(s_hi, w_hi) + (mm(s_lo, w_hi) + mm(s_hi, w_lo))

    def total(bi, out):
        swap = copy(surf.at[bi, c], surf.at[bi, c], bi, 0, other)
        swap.start()
        mine = partial(bi, c)
        swap.wait_recv()
        mine = mine + partial(bi, 1 - c)
        for k in range(HB):
            part[bi, k] = mine[:, k * BLK : (k + 1) * BLK]
        for r, (pq, target) in enumerate(plane):
            rows = pl.ds(pl.multiple_of(pq * ROWS, ROWS), ROWS)
            copy(part.at[bi, :, rows, :], got1.at[bi, r], bi, 1, target).start()
        if bi == 0:
            tapers()
        copy(got1.at[bi], got1.at[bi], bi, 1, other).wait_recv()
        mine = part[bi, :, members, :]
        for r in range(len(plane)):
            mine = mine + got1[bi, r]
        got2[bi, z] = mine
        for target in line:
            copy(got2.at[bi, z], got2.at[bi, z], bi, 2, target).start()
        seven = got2.at[bi, pl.ds(0, NZ - 1)]
        copy(seven, seven, bi, 2, other).wait_recv()
        mine = got2[bi, 0]
        for r in range(1, NZ):
            mine = mine + got2[bi, r]
        out[blocks, members, :] = mine
        own = out.at[blocks, members, :]
        for _, target in plane:
            copy(own, own, bi, 3, target).start()
        copy(got1.at[bi], got1.at[bi], bi, 3, other).wait_recv()
        half = out.at[blocks]
        copy(half, half, bi, 4, other).start()
        copy(half, half, bi, 4, other).wait_recv()

    def tapers():
        lon0 = ((y * NC + c) * CL).astype(F32)
        lat0 = ((x * NZ + z) * CL).astype(F32)
        for k in range(NB):
            lanes = slice(k * BLK, (k + 1) * BLK)
            obs_lat, obs_lon = positions(st, fr, 0, lanes)
            weight = 1.0 / (variance[0:1, lanes] * (MEM - 1.0))
            lon = lax.broadcasted_iota(jnp.int32, (CL, BLK), 0).astype(F32) + lon0
            lon_diff = jnp.abs(lon - obs_lon)
            lon_diff = jnp.minimum(lon_diff, NLON - lon_diff)
            lon_diff = lon_diff * lon_diff

            def one(i, carry):
                lat_diff = (lat0 + lax.convert_element_type(i, F32)) - obs_lat
                distance = jnp.sqrt(lat_diff * lat_diff + lon_diff)
                rows = pl.ds(pl.multiple_of(i * CL, CL), CL)
                taper[rows, lanes] = taper_gc(distance / CL) * weight
                return carry

            lax.fori_loop(0, CL, one, 0)

    pl.semaphore_wait(barrier, len(partners))
    total(0, out0)

    centre(out0, value, 0, anom, packed)
    m, g = normal(anom, 1.0 / variance[0:1, :])
    xy, low = inverse_start(m)
    for _ in range(STEPS):
        xy, low = inverse_step(xy, low)
    factor = spread_factor(inverse_finish(m, xy[0:MEM, :]), g)
    factor_out[...] = factor

    surface = surf[0, c].reshape(CL * CL, MEM)
    a_hi, a_lo = split(surface - jnp.mean(surface, axis=-1, keepdims=True))
    cov = mm(a_hi, packed[0:MEM, :]) + (
        mm(a_lo, packed[0:MEM, :]) + mm(a_hi, packed[MEM : 2 * MEM, :])
    )
    cov_hi, cov_lo = split(cov * taper[...])
    s_hi, s_lo = split(anom[MEM : MEM + 1, :] - dot(factor, anom[0:MEM, :]))
    delta = mm_nt(cov_hi, s_hi) + (mm_nt(cov_lo, s_hi) + mm_nt(cov_hi, s_lo))
    surf[1, c] = (surface + delta).reshape(CL, CL, MEM)

    total(1, out1)

    for bi, out in ((0, out0), (1, out1)):
        copy(surf.at[bi, c], surf.at[bi, c], bi, 0, other).wait_send()
        copy(got1.at[bi], got1.at[bi], bi, 1, other).wait_send()
        seven = got2.at[bi, pl.ds(0, NZ - 1)]
        copy(seven, seven, bi, 2, other).wait_send()
        copy(got1.at[bi], got1.at[bi], bi, 3, other).wait_send()
        copy(out.at[blocks], out.at[blocks], bi, 4, other).wait_send()


def observe(ens, st, fr, value, variance):
    vmem = pl.BlockSpec(memory_space=pltpu.VMEM)
    block = jax.ShapeDtypeStruct((NB, MEM, BLK), F32)
    batches = st.shape[0]
    return pl.pallas_call(
        observe_kernel,
        out_shape=(block, block, jax.ShapeDtypeStruct((MEM, MEM), F32)),
        in_specs=[pl.BlockSpec(memory_space=pltpu.HBM)] * 5,
        out_specs=(vmem, vmem, vmem),
        scratch_shapes=[
            pltpu.VMEM(st.shape, jnp.int32),
            pltpu.VMEM(fr.shape, F32),
            pltpu.VMEM(value.shape, F32),
            pltpu.VMEM(variance.shape, F32),
            pltpu.VMEM((batches, NC, CL, CL, MEM), F32),
            pltpu.VMEM((batches, HB, MEM, BLK), F32),
            pltpu.VMEM((batches, NX * NY - 1, HB, ROWS, BLK), F32),
            pltpu.VMEM((batches, NZ, HB, ROWS, BLK), F32),
            pltpu.VMEM((MEM + 8, NOBS), F32),
            pltpu.VMEM((2 * MEM, NOBS), BF16),
            pltpu.VMEM((CL * CL, NOBS), F32),
            pltpu.SemaphoreType.DMA((5,)),
            pltpu.SemaphoreType.DMA((batches, 5)),
            pltpu.SemaphoreType.DMA((batches, 5)),
        ],
        compiler_params=pltpu.CompilerParams(
            collective_id=0, has_side_effects=True, vmem_limit_bytes=32 << 20
        ),
        name="observe",
    )(ens, st, fr, value, variance)


META = 16


def update_kernel(
    ens, observed0, observed1, factor0, st, fr, value, variance, out,
    anom, packed, chosen, apack, spack, meta, work,
):
    x, y, z, c = place()
    lat0 = ((x * NZ + z) * CL).astype(F32)
    lon0 = ((y * NC + c) * CL).astype(F32)
    all_obs = slice(0, NOBS)

    def select(bi, observed, solve):
        centre(observed, value, bi, anom, packed)
        inv_row = 1.0 / variance[bi : bi + 1, :]
        factor = solve(inv_row)
        obs_lat, obs_lon = positions(st, fr, bi, all_obs)
        half = 0.5 * (CL - 1)
        d_lat = jnp.maximum(jnp.abs(obs_lat - (lat0 + half)) - half, 0.0)
        d_lon = jnp.abs(obs_lon - (lon0 + half))
        d_lon = jnp.maximum(jnp.minimum(d_lon, NLON - d_lon) - half, 0.0)
        reach = 2.0 * CL
        near = jnp.where(d_lat * d_lat + d_lon * d_lon <= reach * reach + 0.5, 1.0, 0.0)
        rows = jnp.concatenate([near[:, k * BLK : (k + 1) * BLK] for k in range(NB)], axis=0)
        before = lax.broadcasted_iota(jnp.int32, (BLK, BLK), 0) < lax.broadcasted_iota(
            jnp.int32, (BLK, BLK), 1
        )
        rank = mm(rows.astype(BF16), jnp.where(before, 1.0, 0.0).astype(BF16))
        count = mm(rows.astype(BF16), jnp.ones((BLK, BLK), BF16))
        offset = jnp.zeros((1, BLK), F32)
        for k in range(NB):
            chosen[k : k + 1, :] = jnp.where(
                rows[k : k + 1, :] > 0.0, rank[k : k + 1, :] + offset, -1.0
            )
            offset = offset + count[k : k + 1, :]
        chunks = (jnp.sum(near).astype(jnp.int32) + (BLK - 1)) // BLK

        zero = jnp.zeros((1, NOBS), BF16)
        lines = [
            *split3(obs_lat), *split3(obs_lon), *split3(inv_row), *split3(anom[MEM : MEM + 1, :])
        ]
        packed[2 * MEM :, :] = jnp.concatenate(lines + [zero] * (META - len(lines)), axis=0)

        def gather(chunk, carry):
            slot = (lax.broadcasted_iota(jnp.int32, (BLK, BLK), 0) + chunk * BLK).astype(F32)
            pick = jnp.concatenate(
                [
                    jnp.where(chosen[k : k + 1, :] == slot, 1.0, 0.0).astype(BF16)
                    for k in range(NB)
                ],
                axis=1,
            )
            got = mm_nt(packed[...], pick)
            near_anom = got[0:MEM] + got[MEM : 2 * MEM]

            def line(k):
                r = 2 * MEM + 3 * k
                return got[r : r + 1] + (got[r + 1 : r + 2] + got[r + 2 : r + 3])

            near_spread = (line(3) - dot(factor, near_anom)).T
            for ref, val in ((apack, near_anom), (spack, near_spread)):
                both = jnp.concatenate(split(val), axis=1)
                ref[bi, chunk, 0:MEM, :] = both
                ref[bi, chunk, MEM:, :] = both
            meta[bi, chunk, 0:1, :] = line(0)
            meta[bi, chunk, 1:2, :] = line(1)
            meta[bi, chunk, 2:3, :] = line(2) / (MEM - 1.0)
            return carry

        lax.fori_loop(0, chunks, gather, 0)
        return chunks

    def solve(inv_row):
        m, g = normal(anom, inv_row)
        xy, low = inverse_start(m)
        work[...] = xy

        def step(low):
            xy, low = inverse_step(work[...], jnp.full((1, 1), low, F32))
            work[...] = xy
            return low[0, 0]

        lax.while_loop(lambda low: low < 0.999, step, low[0, 0])
        return spread_factor(inverse_finish(m, work[0:MEM, :]), g)

    counts = (
        select(0, observed0, lambda inv_row: factor0[...]),
        select(1, observed1, solve),
    )

    def rows_of(step, carry):
        lats = pl.ds(step * TL, TL)
        out[lats] = ens[lats]
        for bi, chunks in enumerate(counts):
            state = out[lats]
            anomaly = state - jnp.mean(state, axis=-1, keepdims=True)
            left = jnp.concatenate(split(anomaly.reshape(TL * CL * DEPTH, MEM)), axis=1)

            def add(chunk, carry):
                lon = lax.broadcasted_iota(jnp.int32, (CL, BLK), 0).astype(F32) + lon0
                lon_diff = jnp.abs(lon - meta[bi, chunk, 1:2, :])
                lon_diff = jnp.minimum(lon_diff, NLON - lon_diff)
                tapers = []
                for i in range(TL):
                    lat_diff = (lat0 + (step * TL + i).astype(F32)) - meta[bi, chunk, 0:1, :]
                    distance = jnp.sqrt(lat_diff * lat_diff + lon_diff * lon_diff)
                    tapers.append(taper_gc(distance / CL) * meta[bi, chunk, 2:3, :])
                taper = jnp.stack(tapers)
                cov = mm(left, apack[bi, chunk])
                cov = (cov[:, 0:BLK] + cov[:, BLK:]).reshape(TL, CL, DEPTH, BLK)
                cov = (cov * taper[:, :, None, :]).reshape(TL * CL * DEPTH, BLK)
                delta = mm(jnp.concatenate(split(cov), axis=1), spack[bi, chunk])
                delta = delta[:, 0:MEM] + delta[:, MEM:]
                out[lats] = out[lats] + delta.reshape(TL, CL, DEPTH, MEM)
                return carry

            lax.fori_loop(0, chunks, add, 0)
        return carry

    lax.fori_loop(0, CL // TL, rows_of, 0)


def update(ens, observed0, observed1, factor0, st, fr, value, variance):
    vmem = pl.BlockSpec(memory_space=pltpu.VMEM)
    batches = st.shape[0]
    return pl.pallas_call(
        update_kernel,
        out_shape=jax.ShapeDtypeStruct(ens.shape, F32),
        in_specs=[vmem] * 8,
        out_specs=vmem,
        scratch_shapes=[
            pltpu.VMEM((MEM + 8, NOBS), F32),
            pltpu.VMEM((2 * MEM + META, NOBS), BF16),
            pltpu.VMEM((NB, BLK), F32),
            pltpu.VMEM((batches, NB, 2 * MEM, 2 * BLK), BF16),
            pltpu.VMEM((batches, NB, 2 * BLK, 2 * MEM), BF16),
            pltpu.VMEM((batches, NB, 8, BLK), F32),
            pltpu.VMEM((2 * MEM, MEM), F32),
        ],
        compiler_params=pltpu.CompilerParams(vmem_limit_bytes=48 << 20),
        name="update",
    )(ens, observed0, observed1, factor0, st, fr, value, variance)


def local(prior, stencil_rows, obs_frac, obs_value, obs_var):
    st = jnp.transpose(stencil_rows, (0, 2, 1))
    fr = jnp.transpose(obs_frac, (0, 2, 1))
    observed0, observed1, factor0 = observe(prior, st, fr, obs_value, obs_var)
    return update(prior, observed0, observed1, factor0, st, fr, obs_value, obs_var)


def solution(mesh):
    placed = (P("lat", "lon", None, None), P(), P(), P(), P())
    return jax.shard_map(
        local, mesh=mesh, in_specs=placed, out_specs=P("lat", "lon", None, None), check_vma=False
    )
```

```python
import functools

import jax
import jax.numpy as jnp
from jax import lax
from jax.experimental import pallas as pl
from jax.experimental.pallas import tpu as pltpu
from jax.sharding import PartitionSpec as P

MESH = pl.DeviceIdType.MESH
F32, BF16 = jnp.float32, jnp.bfloat16
HIGHEST = lax.Precision.HIGHEST
NX, NY, NZ, NC = 4, 4, 8, 2
CL = 16
DEPTH = 16
MEM = 128
NOBS = 1024
NLON = 128
BLK = 128
NB = NOBS // BLK
HB = NB // NC
ROWS = 8
TL = 4
EXACT, PACKED = 4, 7
META = 16


def split(v):
    hi = v.astype(BF16)
    return hi, (v - hi.astype(F32)).astype(BF16)


def split3(v):
    hi = v.astype(BF16)
    rest = v - hi.astype(F32)
    mid = rest.astype(BF16)
    return hi, mid, (rest - mid.astype(F32)).astype(BF16)


def mm(a, b):
    return jnp.dot(a, b, preferred_element_type=F32)


def mm_nt(a, b, precision=None):
    return lax.dot_general(
        a, b, (((1,), (1,)), ((), ())), preferred_element_type=F32, precision=precision
    )


def place():
    lat, lon = lax.axis_index("lat"), lax.axis_index("lon")
    return lat // NZ, lon // NC, lat % NZ, lon % NC


def device(x, y, z, c):
    return (x * NZ + z, y * NC + c)


def eye(scale):
    diagonal = lax.broadcasted_iota(jnp.int32, (MEM, MEM), 0) == lax.broadcasted_iota(
        jnp.int32, (MEM, MEM), 1
    )
    return jnp.where(diagonal, scale, 0.0)


def dot(a, b):
    return jnp.dot(a, b, preferred_element_type=F32, precision=HIGHEST)


def inverse_start(m):
    bound = jnp.max(jnp.sum(jnp.abs(m), axis=0, keepdims=True), axis=1, keepdims=True)
    scale = 1.0 / bound
    return jnp.concatenate([eye(1.0) * scale, m * scale], axis=0), (MEM - 1.0) * scale


def pack_left(v):
    return jnp.concatenate(split(v), axis=1)


def pack_right(v):
    both = jnp.concatenate(split(v), axis=1)
    return jnp.concatenate([both, both], axis=0)


def packed_dot(left, right):
    both = mm(left, right)
    n = both.shape[1] // 2
    return both[:, 0:n] + both[:, n:]


def inverse_step(xy, low, exact):
    s = jnp.minimum(2.0 / (1.0 + low), 1.95)
    z = eye(2.0) * s - xy[MEM:, :] * (s * s)
    t = s * low
    low = jnp.minimum(t * (2.0 - t), s * (2.0 - s))
    return (dot(xy, z) if exact else packed_dot(pack_left(xy), pack_right(z))), low


def inverse_finish(m, x):
    return x + dot(x, eye(1.0) - dot(m, x))


def taper_gc(scaled):
    inner_part = (
        ((-0.25 * scaled + 0.5) * scaled + 0.625) * scaled - 5.0 / 3.0
    ) * scaled * scaled + 1.0
    outer_part = (
        ((((scaled / 12.0 - 0.5) * scaled + 0.625) * scaled + 5.0 / 3.0) * scaled - 5.0) * scaled
        + 4.0
        - 2.0 / (3.0 * jnp.maximum(scaled, 1.0))
    )
    return jnp.where(scaled <= 1.0, inner_part, jnp.where(scaled <= 2.0, outer_part, 0.0))


def positions(st, fr, bi, lanes):
    first = st[bi, 0:1, lanes]
    obs_lat = lax.shift_right_logical(first, 11).astype(F32) + fr[bi, 0:1, lanes]
    obs_lon = (lax.shift_right_logical(first, 4) & (NLON - 1)).astype(F32) + fr[bi, 1:2, lanes]
    return obs_lat, obs_lon


def meta_lines(st, fr, variance, bi, lanes, width, innovation):
    obs_lat, obs_lon = positions(st, fr, bi, lanes)
    weight = 1.0 / variance[bi : bi + 1, lanes]
    lines = [*split3(obs_lat), *split3(obs_lon), *split3(weight), *split3(innovation)]
    zero = jnp.zeros((META - len(lines), width), BF16)
    return jnp.concatenate(lines + [zero], axis=0)


def join(got, row):
    return got[row : row + 1] + (got[row + 1 : row + 2] + got[row + 2 : row + 3])


def lon_distance(lon0, obs_lon):
    lon = lax.broadcasted_iota(jnp.int32, (CL, BLK), 0).astype(F32) + lon0
    lon_diff = jnp.abs(lon - obs_lon)
    lon_diff = jnp.minimum(lon_diff, NLON - lon_diff)
    return lon_diff * lon_diff


def lat_taper(lat, obs_lat, lon_diff, weight):
    lat_diff = lat - obs_lat
    return taper_gc(jnp.sqrt(lat_diff * lat_diff + lon_diff) / CL) * weight


def spread_factor(inv, g):
    return (0.5 * (MEM - 1.0)) * inv + jnp.sum(inv * g, axis=0, keepdims=True)


def one_hot(chosen, chunk):
    slot = (lax.broadcasted_iota(jnp.int32, (BLK, BLK), 0) + chunk * BLK).astype(F32)
    return jnp.concatenate(
        [jnp.where(chosen[k : k + 1, :] == slot, 1.0, 0.0).astype(BF16) for k in range(NB)],
        axis=1,
    )


def gather(packed, pick, factor):
    got = mm_nt(packed, pick)
    near_anom = got[0:MEM] + got[MEM : 2 * MEM]
    lines = got[2 * MEM :]
    near_spread = (join(lines, 9) - dot(factor, near_anom)).T
    return pack_right(near_anom), pack_right(near_spread), lines


def increment(state, apack, spack, taper):
    rows = state.shape[0] * CL * DEPTH
    anomaly = state - jnp.mean(state, axis=-1, keepdims=True)
    cov = packed_dot(pack_left(anomaly.reshape(rows, MEM)), apack)
    cov = cov.reshape(state.shape[0], CL, DEPTH, BLK) * taper[:, :, None, :]
    return packed_dot(pack_left(cov.reshape(rows, BLK)), spack).reshape(state.shape)


def observe_kernel(
    ens_in, st_in, fr_in, value_in, var_in,
    ens, packed, chosen, pick1, taper1, gram_out, factor_out,
    state, st, fr, value, variance, surf, part, got1, got2, observed, anom, taper, pick0, taper0,
    apack, spack, load, send, recv,
):
    x, y, z, c = place()
    q = x * NY + y
    lat0 = ((x * NZ + z) * CL).astype(F32)
    lon0 = ((y * NC + c) * CL).astype(F32)
    plane = []
    for r in range(1, NX * NY):
        px, py = lax.rem(x + r // NY, NX), lax.rem(y + r % NY, NY)
        plane.append((px * NY + py, device(px, py, z, c)))
    line = [device(x, y, lax.rem(z + r, NZ), c) for r in range(1, NZ)]
    other = device(x, y, z, 1 - c)

    def copy(src, dst, bi, stage, target):
        return pltpu.make_async_remote_copy(
            src_ref=src,
            dst_ref=dst,
            send_sem=send.at[bi, stage],
            recv_sem=recv.at[bi, stage],
            device_id=target,
            device_id_type=MESH,
        )

    barrier = pltpu.get_barrier_semaphore()
    partners = [other] + [d for _, d in plane] + line
    loads = [
        pltpu.make_async_copy(ens_in.at[:, :, 0, :], surf.at[0, c], load.at[0]),
        pltpu.make_async_copy(st_in, st, load.at[1]),
        pltpu.make_async_copy(fr_in, fr, load.at[2]),
        pltpu.make_async_copy(value_in, value, load.at[3]),
        pltpu.make_async_copy(var_in, variance, load.at[4]),
        pltpu.make_async_copy(ens_in, state, load.at[5]),
    ]
    for one in loads:
        one.start()
    for target in partners:
        pl.semaphore_signal(barrier, inc=1, device_id=target, device_id_type=MESH)
    for one in loads[:-1]:
        one.wait()

    def span_of(core):
        return pl.ds(pl.multiple_of(core * (HB * BLK), BLK), HB * BLK)

    span = span_of(c)
    cells = lax.broadcasted_iota(jnp.int32, (CL, HB * BLK), 0)
    members = pl.ds(pl.multiple_of(q * ROWS, ROWS), ROWS)
    blocks = pl.ds(c * HB, HB)

    def partial(bi, core):
        first = st[bi, 0:1, span]
        base_lat = lax.shift_right_logical(first, 11)
        base_lon = lax.shift_right_logical(first, 4) & (NLON - 1)
        east = (base_lon + 1) & (NLON - 1)
        fa, fo = fr[bi, 0:1, span], fr[bi, 1:2, span]
        lat = cells + (x * NZ + z) * CL
        lon = cells + (y * NC + core) * CL
        w_lat = jnp.where(lat == base_lat, 1.0 - fa, jnp.where(lat == base_lat + 1, fa, 0.0))
        w_lon = jnp.where(lon == base_lon, 1.0 - fo, jnp.where(lon == east, fo, 0.0))
        w = (w_lat[:, None, :] * w_lon[None, :, :]).reshape(CL * CL, HB * BLK)
        s_hi, s_lo = split(surf[bi, core].reshape(CL * CL, MEM).T)
        w_hi, w_lo = split(w)
        return mm(s_hi, w_hi) + (mm(s_lo, w_hi) + mm(s_hi, w_lo))

    def tapers():
        for k in range(NB):
            lanes = slice(k * BLK, (k + 1) * BLK)
            obs_lat, obs_lon = positions(st, fr, 0, lanes)
            weight = 1.0 / (variance[0:1, lanes] * (MEM - 1.0))
            lon_diff = lon_distance(lon0, obs_lon)

            def one(i, carry):
                rows = pl.ds(pl.multiple_of(i * CL, CL), CL)
                lat = lat0 + lax.convert_element_type(i, F32)
                taper[rows, lanes] = lat_taper(lat, obs_lat, lon_diff, weight)
                return carry

            lax.fori_loop(0, CL, one, 0)

    def select(bi, pick, near_taper):
        obs_lat, obs_lon = positions(st, fr, bi, slice(0, NOBS))
        half = 0.5 * (CL - 1)
        d_lat = jnp.maximum(jnp.abs(obs_lat - (lat0 + half)) - half, 0.0)
        d_lon = jnp.abs(obs_lon - (lon0 + half))
        d_lon = jnp.maximum(jnp.minimum(d_lon, NLON - d_lon) - half, 0.0)
        reach = 2.0 * CL
        near = jnp.where(d_lat * d_lat + d_lon * d_lon <= reach * reach + 0.5, 1.0, 0.0)
        rows = jnp.concatenate([near[:, k * BLK : (k + 1) * BLK] for k in range(NB)], axis=0)
        before = lax.broadcasted_iota(jnp.int32, (BLK, BLK), 0) < lax.broadcasted_iota(
            jnp.int32, (BLK, BLK), 1
        )
        rank = mm(rows.astype(BF16), jnp.where(before, 1.0, 0.0).astype(BF16))
        count = mm(rows.astype(BF16), jnp.ones((BLK, BLK), BF16))
        offset = jnp.zeros((1, BLK), F32)
        for k in range(NB):
            chosen[bi, k : k + 1, :] = jnp.where(
                rows[k : k + 1, :] > 0.0, rank[k : k + 1, :] + offset, -1.0
            )
            offset = offset + count[k : k + 1, :]
        pick[...] = one_hot(chosen[bi], 0)
        lines = meta_lines(st, fr, variance, bi, slice(0, NOBS), NOBS, jnp.zeros((1, NOBS), F32))
        got = mm_nt(lines, pick[...])
        lon_diff = lon_distance(lon0, join(got, 3))
        weight = join(got, 6) / (MEM - 1.0)
        for i in range(CL):
            near_taper[i] = lat_taper(lat0 + i, join(got, 0), lon_diff, weight)

    def update_all():
        loads[-1].wait()
        a, s, _ = gather(packed[0], pick0[...], factor_out[...])
        apack[...] = a
        spack[...] = s

        def rows_of(step, carry):
            lats = pl.ds(step * TL, TL)
            old = state[lats]
            ens[lats] = old + increment(old, apack[...], spack[...], taper0[lats])
            return carry

        lax.fori_loop(0, CL // TL, rows_of, 0)

    def centre(bi, core):
        half = span_of(core)
        for k in range(HB):
            lanes = pl.ds(pl.multiple_of((core * HB + k) * BLK, BLK), BLK)
            block = observed[bi, core * HB + k]
            mean = jnp.sum(block, axis=0, keepdims=True) / MEM
            block = block - mean
            innovation = value[bi : bi + 1, lanes] - mean
            anom[0:MEM, lanes] = block
            anom[MEM : MEM + 8, lanes] = jnp.broadcast_to(innovation, (8, BLK))
            hi, lo = split(block)
            packed[bi, 0:MEM, lanes] = hi
            packed[bi, MEM : 2 * MEM, lanes] = lo
            packed[bi, 2 * MEM :, lanes] = meta_lines(st, fr, variance, bi, lanes, BLK, innovation)
        weight = 1.0 / variance[bi : bi + 1, half]
        return mm_nt(anom[0:MEM, half] * weight, anom[:, half], HIGHEST)

    def total(bi, mine, swap):
        swap.wait_recv()
        mine = mine + partial(bi, 1 - c)
        for k in range(HB):
            part[bi, k] = mine[:, k * BLK : (k + 1) * BLK]
        for r, (pq, target) in enumerate(plane):
            rows = pl.ds(pl.multiple_of(pq * ROWS, ROWS), ROWS)
            copy(part.at[bi, :, rows, :], got1.at[bi, r], bi, 1, target).start()
        if bi == 0:
            tapers()
        else:
            update_all()
        copy(got1.at[bi], got1.at[bi], bi, 1, other).wait_recv()
        mine = part[bi, :, members, :]
        for r in range(len(plane)):
            mine = mine + got1[bi, r]
        got2[bi, z] = mine
        for target in line:
            copy(got2.at[bi, z], got2.at[bi, z], bi, 2, target).start()
        if bi == 0:
            select(0, pick0, taper0)
        seven = got2.at[bi, pl.ds(0, NZ - 1)]
        copy(seven, seven, bi, 2, other).wait_recv()
        mine = got2[bi, 0]
        for r in range(1, NZ):
            mine = mine + got2[bi, r]
        observed[bi, blocks, members, :] = mine
        own = observed.at[bi, blocks, members, :]
        for _, target in plane:
            copy(own, own, bi, 3, target).start()
        if bi == 0:
            select(1, pick1, taper1)
        copy(got1.at[bi], got1.at[bi], bi, 3, other).wait_recv()
        half = observed.at[bi, blocks]
        copy(half, half, bi, 4, other).start()
        gram = centre(bi, c)
        copy(half, half, bi, 4, other).wait_recv()
        return gram + centre(bi, 1 - c)

    def swap_of(bi):
        return copy(surf.at[bi, c], surf.at[bi, c], bi, 0, other)

    mine = partial(0, c)
    pl.semaphore_wait(barrier, len(partners))
    swap_of(0).start()
    gram = total(0, mine, swap_of(0))

    m = gram[:, 0:MEM] + eye(MEM - 1.0)
    xy, low = inverse_start(m)
    for i in range(EXACT + PACKED):
        xy, low = inverse_step(xy, low, i < EXACT)
    factor = spread_factor(inverse_finish(m, xy[0:MEM, :]), gram[:, MEM : MEM + 1])
    factor_out[...] = factor

    surface = surf[0, c].reshape(CL * CL, MEM)
    a_hi, a_lo = split(surface - jnp.mean(surface, axis=-1, keepdims=True))
    b_hi, b_lo = packed[0, 0:MEM, :], packed[0, MEM : 2 * MEM, :]
    cov = mm(a_hi, b_hi) + (mm(a_lo, b_hi) + mm(a_hi, b_lo))
    cov_hi, cov_lo = split(cov * taper[...])
    s_hi, s_lo = split(anom[MEM : MEM + 1, :] - dot(factor, anom[0:MEM, :]))
    delta = mm_nt(cov_hi, s_hi) + (mm_nt(cov_lo, s_hi) + mm_nt(cov_hi, s_lo))
    surf[1, c] = (surface + delta).reshape(CL, CL, MEM)

    swap_of(1).start()
    gram_out[...] = total(1, partial(1, c), swap_of(1))

    for bi in range(2):
        swap_of(bi).wait_send()
        copy(got1.at[bi], got1.at[bi], bi, 1, other).wait_send()
        seven = got2.at[bi, pl.ds(0, NZ - 1)]
        copy(seven, seven, bi, 2, other).wait_send()
        copy(got1.at[bi], got1.at[bi], bi, 3, other).wait_send()
        copy(observed.at[bi, blocks], observed.at[bi, blocks], bi, 4, other).wait_send()


def in_hbm(*arrays):
    return [pltpu.with_memory_space_constraint(a, pltpu.HBM) for a in arrays]


def observe(ens, st, fr, value, variance):
    batches = st.shape[0]
    outs = (
        (ens.shape, F32),
        ((batches, 2 * MEM + META, NOBS), BF16),
        ((batches, NB, BLK), F32),
        ((BLK, NOBS), BF16),
        ((CL, CL, BLK), F32),
        ((MEM, MEM + 8), F32),
        ((MEM, MEM), F32),
    )
    return pl.pallas_call(
        observe_kernel,
        out_shape=tuple(jax.ShapeDtypeStruct(*o) for o in outs),
        in_specs=[pl.BlockSpec(memory_space=pltpu.HBM)] * 5,
        out_specs=tuple(pl.BlockSpec(memory_space=pltpu.VMEM) for _ in outs),
        scratch_shapes=[
            pltpu.VMEM(ens.shape, F32),
            pltpu.VMEM(st.shape, jnp.int32),
            pltpu.VMEM(fr.shape, F32),
            pltpu.VMEM(value.shape, F32),
            pltpu.VMEM(variance.shape, F32),
            pltpu.VMEM((batches, NC, CL, CL, MEM), F32),
            pltpu.VMEM((batches, HB, MEM, BLK), F32),
            pltpu.VMEM((batches, NX * NY - 1, HB, ROWS, BLK), F32),
            pltpu.VMEM((batches, NZ, HB, ROWS, BLK), F32),
            pltpu.VMEM((batches, NB, MEM, BLK), F32),
            pltpu.VMEM((MEM + 8, NOBS), F32),
            pltpu.VMEM((CL * CL, NOBS), F32),
            pltpu.VMEM((BLK, NOBS), BF16),
            pltpu.VMEM((CL, CL, BLK), F32),
            pltpu.VMEM((2 * MEM, 2 * BLK), BF16),
            pltpu.VMEM((2 * BLK, 2 * MEM), BF16),
            pltpu.SemaphoreType.DMA((6,)),
            pltpu.SemaphoreType.DMA((batches, 5)),
            pltpu.SemaphoreType.DMA((batches, 5)),
        ],
        compiler_params=pltpu.CompilerParams(
            collective_id=0, has_side_effects=True, vmem_limit_bytes=36 << 20
        ),
        name="observe",
    )(*in_hbm(ens, st, fr, value, variance))


def update_kernel(
    prior, ens, packed, chosen, pick1, taper1, gram, factor0, out,
    work, factor1, apack, spack, taper, base, staged, sems,
):
    x, y, z, c = place()
    lat0 = ((x * NZ + z) * CL).astype(F32)
    lon0 = ((y * NC + c) * CL).astype(F32)

    m = gram[:, 0:MEM] + eye(MEM - 1.0)
    xy, low = inverse_start(m)
    work[...] = xy

    def step(exact, low):
        xy, low = inverse_step(work[...], jnp.full((1, 1), low, F32), exact)
        work[...] = xy
        return low[0, 0]

    low = lax.while_loop(lambda v: v < 0.001, functools.partial(step, True), low[0, 0])
    lax.while_loop(lambda v: v < 0.999, functools.partial(step, False), low)
    factor1[...] = spread_factor(inverse_finish(m, work[0:MEM, :]), gram[:, MEM : MEM + 1])

    def chunks_of(bi):
        return (jnp.max(chosen[bi]).astype(jnp.int32) + BLK) // BLK

    chunks = chunks_of(0), chunks_of(1)
    short = jnp.maximum(chunks[0], chunks[1]) <= 1

    def rest(bi, start, factor):
        def one(chunk, carry):
            a, s, lines = gather(packed[bi], one_hot(chosen[bi], chunk), factor[...])
            apack[...] = a
            spack[...] = s
            lon_diff = lon_distance(lon0, join(lines, 3))
            weight = join(lines, 6) / (MEM - 1.0)
            for i in range(CL):
                taper[i] = lat_taper(lat0 + i, join(lines, 0), lon_diff, weight)

            def rows_of(step, carry):
                lats = pl.ds(step * TL, TL)
                staged[lats] += increment(base[lats], apack[...], spack[...], taper[lats])
                return carry

            lax.fori_loop(0, CL // TL, rows_of, 0)
            return carry

        lax.fori_loop(start, chunks[bi], one, 0)

    @pl.when(short)
    def _():
        a, s, _ = gather(packed[1], pick1[...], factor1[...])
        apack[...] = a
        spack[...] = s
        writes = []
        for i in range(CL // TL):
            lats = slice(i * TL, (i + 1) * TL)
            old = ens[lats]
            staged[lats] = old + increment(old, apack[...], spack[...], taper1[lats])
            writes.append(pltpu.make_async_copy(staged.at[lats], out.at[lats], sems.at[i]))
            writes[-1].start()
        for one in writes:
            one.wait()

    @pl.when(jnp.logical_not(short))
    def _():
        pltpu.sync_copy(prior, base)
        staged[...] = ens[...]
        rest(0, 1, factor0)
        base[...] = staged[...]
        rest(1, 0, factor1)
        pltpu.sync_copy(staged, out)


def update(prior, ens, packed, chosen, pick1, taper1, gram, factor0):
    vmem = pl.BlockSpec(memory_space=pltpu.VMEM)
    hbm = pl.BlockSpec(memory_space=pltpu.HBM)
    return pl.pallas_call(
        update_kernel,
        out_shape=jax.ShapeDtypeStruct(prior.shape, F32),
        in_specs=[hbm] + [vmem] * 7,
        out_specs=hbm,
        scratch_shapes=[
            pltpu.VMEM((2 * MEM, MEM), F32),
            pltpu.VMEM((MEM, MEM), F32),
            pltpu.VMEM((2 * MEM, 2 * BLK), BF16),
            pltpu.VMEM((2 * BLK, 2 * MEM), BF16),
            pltpu.VMEM((CL, CL, BLK), F32),
            pltpu.VMEM(prior.shape, F32),
            pltpu.VMEM(prior.shape, F32),
            pltpu.SemaphoreType.DMA((CL // TL,)),
        ],
        compiler_params=pltpu.CompilerParams(vmem_limit_bytes=40 << 20),
        name="update",
    )(*in_hbm(prior), ens, packed, chosen, pick1, taper1, gram, factor0)


def local(prior, stencil_rows, obs_frac, obs_value, obs_var):
    st = jnp.transpose(stencil_rows, (0, 2, 1))
    fr = jnp.transpose(obs_frac, (0, 2, 1))
    return update(prior, *observe(prior, st, fr, obs_value, obs_var))


def solution(mesh):
    placed = (P("lat", "lon", None, None), P(), P(), P(), P())
    return jax.shard_map(
        local, mesh=mesh, in_specs=placed, out_specs=P("lat", "lon", None, None), check_vma=False
    )
```

```python
import functools

import jax
import jax.numpy as jnp
from jax import lax
from jax.experimental import pallas as pl
from jax.experimental.pallas import tpu as pltpu
from jax.sharding import PartitionSpec as P

MESH = pl.DeviceIdType.MESH
F32, BF16 = jnp.float32, jnp.bfloat16
HIGHEST = lax.Precision.HIGHEST
NX, NY, NZ, NC = 4, 4, 8, 2
CL = 16
DEPTH = 16
MEM = 128
NOBS = 1024
NLON = 128
BLK = 128
NB = NOBS // BLK
HB = NB // NC
ROWS = 8
TL = 4
EXACT, PACKED = 2, 9
META = 16


def split(v):
    hi = v.astype(BF16)
    return hi, (v - hi.astype(F32)).astype(BF16)


def split3(v):
    hi = v.astype(BF16)
    rest = v - hi.astype(F32)
    mid = rest.astype(BF16)
    return hi, mid, (rest - mid.astype(F32)).astype(BF16)


def mm(a, b):
    return jnp.dot(a, b, preferred_element_type=F32)


def mm_nt(a, b, precision=None):
    return lax.dot_general(
        a, b, (((1,), (1,)), ((), ())), preferred_element_type=F32, precision=precision
    )


def place():
    lat, lon = lax.axis_index("lat"), lax.axis_index("lon")
    return lat // NZ, lon // NC, lat % NZ, lon % NC


def hops(step, size):
    return min(step, size - step)


def device(x, y, z, c):
    return (x * NZ + z, y * NC + c)


def eye(scale):
    diagonal = lax.broadcasted_iota(jnp.int32, (MEM, MEM), 0) == lax.broadcasted_iota(
        jnp.int32, (MEM, MEM), 1
    )
    return jnp.where(diagonal, scale, 0.0)


def dot(a, b):
    return jnp.dot(a, b, preferred_element_type=F32, precision=HIGHEST)


def inverse_start(m):
    bound = jnp.max(jnp.sum(jnp.abs(m), axis=0, keepdims=True), axis=1, keepdims=True)
    scale = 1.0 / bound
    return eye(1.0) * scale, m * scale, (MEM - 1.0) * scale


def pack_left(v):
    return jnp.concatenate(split(v), axis=1)


def pack_right(v):
    both = jnp.concatenate(split(v), axis=1)
    return jnp.concatenate([both, both], axis=0)


def packed_dot(left, right):
    both = mm(left, right)
    n = both.shape[1] // 2
    return both[:, 0:n] + both[:, n:]


def inverse_step(x, y, low, exact):
    s = jnp.minimum(2.0 / (1.0 + low), 1.95)
    z = eye(2.0) * s - y * (s * s)
    t = s * low
    low = jnp.minimum(t * (2.0 - t), s * (2.0 - s))
    if exact:
        return dot(x, z), dot(y, z), low
    right = pack_right(z)
    return packed_dot(pack_left(x), right), packed_dot(pack_left(y), right), low


def inverse_finish(m, x):
    return x + dot(x, eye(1.0) - dot(m, x))


def taper_gc(scaled):
    inner_part = (
        ((-0.25 * scaled + 0.5) * scaled + 0.625) * scaled - 5.0 / 3.0
    ) * scaled * scaled + 1.0
    outer_part = (
        ((((scaled / 12.0 - 0.5) * scaled + 0.625) * scaled + 5.0 / 3.0) * scaled - 5.0) * scaled
        + 4.0
        - 2.0 / (3.0 * jnp.maximum(scaled, 1.0))
    )
    return jnp.where(scaled <= 1.0, inner_part, jnp.where(scaled <= 2.0, outer_part, 0.0))


def positions(st, fr, bi, lanes):
    first = st[bi, 0:1, lanes]
    obs_lat = lax.shift_right_logical(first, 11).astype(F32) + fr[bi, 0:1, lanes]
    obs_lon = (lax.shift_right_logical(first, 4) & (NLON - 1)).astype(F32) + fr[bi, 1:2, lanes]
    return obs_lat, obs_lon


def meta_lines(st, fr, variance, bi, lanes, width, innovation):
    obs_lat, obs_lon = positions(st, fr, bi, lanes)
    weight = 1.0 / variance[bi : bi + 1, lanes]
    lines = [*split3(obs_lat), *split3(obs_lon), *split3(weight), *split3(innovation)]
    zero = jnp.zeros((META - len(lines), width), BF16)
    return jnp.concatenate(lines + [zero], axis=0)


def join(got, row):
    return got[row : row + 1] + (got[row + 1 : row + 2] + got[row + 2 : row + 3])


def lon_distance(lon0, obs_lon):
    lon = lax.broadcasted_iota(jnp.int32, (CL, BLK), 0).astype(F32) + lon0
    lon_diff = jnp.abs(lon - obs_lon)
    lon_diff = jnp.minimum(lon_diff, NLON - lon_diff)
    return lon_diff * lon_diff


def lat_taper(lat, obs_lat, lon_diff, weight):
    lat_diff = lat - obs_lat
    return taper_gc(jnp.sqrt(lat_diff * lat_diff + lon_diff) / CL) * weight


def spread_factor(inv, g):
    return (0.5 * (MEM - 1.0)) * inv + jnp.sum(inv * g, axis=0, keepdims=True)


def one_hot(chosen, chunk):
    slot = (lax.broadcasted_iota(jnp.int32, (BLK, BLK), 0) + chunk * BLK).astype(F32)
    return jnp.concatenate(
        [jnp.where(chosen[k : k + 1, :] == slot, 1.0, 0.0).astype(BF16) for k in range(NB)],
        axis=1,
    )


def gather(packed, pick, factor):
    got = mm_nt(packed, pick)
    near_anom = got[0:MEM] + got[MEM : 2 * MEM]
    lines = got[2 * MEM :]
    near_spread = (join(lines, 9) - dot(factor, near_anom)).T
    return pack_right(near_anom), pack_right(near_spread), lines


def increment(state, apack, spack, taper):
    rows = state.shape[0] * CL * DEPTH
    anomaly = state - jnp.mean(state, axis=-1, keepdims=True)
    cov = packed_dot(pack_left(anomaly.reshape(rows, MEM)), apack)
    cov = cov.reshape(state.shape[0], CL, DEPTH, BLK) * taper[:, :, None, :]
    return packed_dot(pack_left(cov.reshape(rows, BLK)), spack).reshape(state.shape)


def observe_kernel(
    ens_in, st_in, fr_in, value_in, var_in,
    ens, packed, chosen, pick1, taper1, gram_out, factor_out,
    state, st, fr, value, variance, surf, part, got1, got2, observed, anom, taper, pick0, taper0,
    apack, spack, wts, gram, load, send, recv,
):
    x, y, z, c = place()
    q = x * NY + y
    lat0 = ((x * NZ + z) * CL).astype(F32)
    lon0 = ((y * NC + c) * CL).astype(F32)
    plane = []
    far = sorted(range(1, NX * NY), key=lambda r: -hops(r // NY, NX) - hops(r % NY, NY))
    for r in far:
        px, py = lax.rem(x + r // NY, NX), lax.rem(y + r % NY, NY)
        plane.append((px * NY + py, device(px, py, z, c)))
    far = sorted(range(1, NZ), key=lambda r: -hops(r, NZ))
    line = [device(x, y, lax.rem(z + r, NZ), c) for r in far]
    other = device(x, y, z, 1 - c)

    def copy(src, dst, bi, stage, target):
        return pltpu.make_async_remote_copy(
            src_ref=src,
            dst_ref=dst,
            send_sem=send.at[bi, stage],
            recv_sem=recv.at[bi, stage],
            device_id=target,
            device_id_type=MESH,
        )

    barrier = pltpu.get_barrier_semaphore()
    partners = line + [d for _, d in plane] + [other]
    for target in partners:
        pl.semaphore_signal(barrier, inc=1, device_id=target, device_id_type=MESH)
    loads = [
        pltpu.make_async_copy(ens_in.at[:, :, 0, :], surf.at[0, c], load.at[0]),
        pltpu.make_async_copy(st_in, st, load.at[1]),
        pltpu.make_async_copy(fr_in, fr, load.at[2]),
        pltpu.make_async_copy(value_in, value, load.at[3]),
        pltpu.make_async_copy(var_in, variance, load.at[4]),
        pltpu.make_async_copy(ens_in, state, load.at[5]),
    ]
    for one in loads:
        one.start()
    for one in loads[:-1]:
        one.wait()

    def span_of(core):
        return pl.ds(pl.multiple_of(core * (HB * BLK), BLK), HB * BLK)

    span = span_of(c)
    cells = lax.broadcasted_iota(jnp.int32, (CL, HB * BLK), 0)
    members = pl.ds(pl.multiple_of(q * ROWS, ROWS), ROWS)
    blocks = pl.ds(c * HB, HB)

    def weights(bi, core):
        first = st[bi, 0:1, span]
        base_lat = lax.shift_right_logical(first, 11)
        base_lon = lax.shift_right_logical(first, 4) & (NLON - 1)
        east = (base_lon + 1) & (NLON - 1)
        fa, fo = fr[bi, 0:1, span], fr[bi, 1:2, span]
        lat = cells + (x * NZ + z) * CL
        lon = cells + (y * NC + core) * CL
        w_lat = jnp.where(lat == base_lat, 1.0 - fa, jnp.where(lat == base_lat + 1, fa, 0.0))
        w_lon = jnp.where(lon == base_lon, 1.0 - fo, jnp.where(lon == east, fo, 0.0))
        return split((w_lat[:, None, :] * w_lon[None, :, :]).reshape(CL * CL, HB * BLK))

    def partial(bi, core):
        w_hi, w_lo = weights(bi, core) if bi == 0 else (wts[core, 0], wts[core, 1])
        s_hi, s_lo = split(surf[bi, core].reshape(CL * CL, MEM).T)
        return mm(s_hi, w_hi) + (mm(s_lo, w_hi) + mm(s_hi, w_lo))

    def tapers():
        for k in range(NB):
            lanes = slice(k * BLK, (k + 1) * BLK)
            obs_lat, obs_lon = positions(st, fr, 0, lanes)
            weight = 1.0 / (variance[0:1, lanes] * (MEM - 1.0))
            lon_diff = lon_distance(lon0, obs_lon)

            def one(i, carry):
                rows = pl.ds(pl.multiple_of(i * CL, CL), CL)
                lat = lat0 + lax.convert_element_type(i, F32)
                taper[rows, lanes] = lat_taper(lat, obs_lat, lon_diff, weight)
                return carry

            lax.fori_loop(0, CL, one, 0)

    def select(bi, pick, near_taper):
        obs_lat, obs_lon = positions(st, fr, bi, slice(0, NOBS))
        half = 0.5 * (CL - 1)
        d_lat = jnp.maximum(jnp.abs(obs_lat - (lat0 + half)) - half, 0.0)
        d_lon = jnp.abs(obs_lon - (lon0 + half))
        d_lon = jnp.maximum(jnp.minimum(d_lon, NLON - d_lon) - half, 0.0)
        reach = 2.0 * CL
        near = jnp.where(d_lat * d_lat + d_lon * d_lon <= reach * reach + 0.5, 1.0, 0.0)
        rows = jnp.concatenate([near[:, k * BLK : (k + 1) * BLK] for k in range(NB)], axis=0)
        before = lax.broadcasted_iota(jnp.int32, (BLK, BLK), 0) < lax.broadcasted_iota(
            jnp.int32, (BLK, BLK), 1
        )
        rank = mm(rows.astype(BF16), jnp.where(before, 1.0, 0.0).astype(BF16))
        count = mm(rows.astype(BF16), jnp.ones((BLK, BLK), BF16))
        offset = jnp.zeros((1, BLK), F32)
        for k in range(NB):
            chosen[bi, k : k + 1, :] = jnp.where(
                rows[k : k + 1, :] > 0.0, rank[k : k + 1, :] + offset, -1.0
            )
            offset = offset + count[k : k + 1, :]
        pick[...] = one_hot(chosen[bi], 0)
        lines = meta_lines(st, fr, variance, bi, slice(0, NOBS), NOBS, jnp.zeros((1, NOBS), F32))
        got = mm_nt(lines, pick[...])
        lon_diff = lon_distance(lon0, join(got, 3))
        weight = join(got, 6) / (MEM - 1.0)
        for i in range(CL):
            near_taper[i] = lat_taper(lat0 + i, join(got, 0), lon_diff, weight)

    def update_all():
        loads[-1].wait()
        a, s, _ = gather(packed[0], pick0[...], factor_out[...])
        apack[...] = a
        spack[...] = s

        def rows_of(step, carry):
            lats = pl.ds(step * TL, TL)
            old = state[lats]
            ens[lats] = old + increment(old, apack[...], spack[...], taper0[lats])
            return carry

        lax.fori_loop(0, CL // TL, rows_of, 0)

    def centre(bi, core):
        for k in range(HB):
            lanes = pl.ds(pl.multiple_of((core * HB + k) * BLK, BLK), BLK)
            block = observed[bi, core * HB + k]
            mean = jnp.sum(block, axis=0, keepdims=True) / MEM
            block = block - mean
            innovation = value[bi : bi + 1, lanes] - mean
            anom[0:MEM, lanes] = block
            anom[MEM : MEM + 8, lanes] = jnp.broadcast_to(innovation, (8, BLK))
            hi, lo = split(block)
            packed[bi, 0:MEM, lanes] = hi
            packed[bi, MEM : 2 * MEM, lanes] = lo
            packed[bi, 2 * MEM :, lanes] = meta_lines(st, fr, variance, bi, lanes, BLK, innovation)

    def surface_sums(core):
        half = span_of(core)
        b_hi, b_lo = packed[0, 0:MEM, half], packed[0, MEM : 2 * MEM, half]
        cov = mm(a_hi, b_hi) + (mm(a_lo, b_hi) + mm(a_hi, b_lo))
        return mm_nt(cov * taper[:, half], anom[:, half], HIGHEST)

    def total(bi, mine, swap):
        swap.wait_recv()
        mine = mine + partial(bi, 1 - c)
        for k in range(HB):
            part[bi, k] = mine[:, k * BLK : (k + 1) * BLK]
        for r, (pq, target) in enumerate(plane):
            rows = pl.ds(pl.multiple_of(pq * ROWS, ROWS), ROWS)
            copy(part.at[bi, :, rows, :], got1.at[bi, r], bi, 1, target).start()
        if bi == 0:
            tapers()
        else:
            update_all()
        copy(got1.at[bi], got1.at[bi], bi, 1, other).wait_recv()
        mine = part[bi, :, members, :]
        for r in range(len(plane)):
            mine = mine + got1[bi, r]
        got2[bi, z] = mine
        for target in line:
            copy(got2.at[bi, z], got2.at[bi, z], bi, 2, target).start()
        if bi == 0:
            select(0, pick0, taper0)
        seven = got2.at[bi, pl.ds(0, NZ - 1)]
        copy(seven, seven, bi, 2, other).wait_recv()
        mine = got2[bi, 0]
        for r in range(1, NZ):
            mine = mine + got2[bi, r]
        observed[bi, blocks, members, :] = mine
        own = observed.at[bi, blocks, members, :]
        for _, target in plane:
            copy(own, own, bi, 3, target).start()
        if bi == 0:
            select(1, pick1, taper1)
            for core in range(NC):
                wts[core, 0], wts[core, 1] = weights(1, core)
        copy(got1.at[bi], got1.at[bi], bi, 3, other).wait_recv()
        half = observed.at[bi, blocks]
        copy(half, half, bi, 4, other).start()
        centre(bi, c)
        weight = 1.0 / variance[bi : bi + 1, span]
        gram[bi, c] = mm_nt(anom[0:MEM, span] * weight, anom[:, span], HIGHEST)
        copy(gram.at[bi, c], gram.at[bi, c], bi, 5, other).start()
        sums = surface_sums(c) if bi == 0 else None
        copy(half, half, bi, 4, other).wait_recv()
        centre(bi, 1 - c)
        copy(gram.at[bi, c], gram.at[bi, c], bi, 5, other).wait_recv()
        if bi == 0:
            sums = sums + surface_sums(1 - c)
        return gram[bi, 0] + gram[bi, 1], sums

    def swap_of(bi):
        return copy(surf.at[bi, c], surf.at[bi, c], bi, 0, other)

    mine = partial(0, c)
    surface = surf[0, c].reshape(CL * CL, MEM)
    a_hi, a_lo = split(surface - jnp.mean(surface, axis=-1, keepdims=True))
    pl.semaphore_wait(barrier, len(partners))
    swap_of(0).start()
    normal, sums = total(0, mine, swap_of(0))

    m = normal[:, 0:MEM] + eye(MEM - 1.0)
    x_now, y_now, low = inverse_start(m)
    for i in range(EXACT + PACKED):
        x_now, y_now, low = inverse_step(x_now, y_now, low, i < EXACT)
    factor = spread_factor(inverse_finish(m, x_now), normal[:, MEM : MEM + 1])
    factor_out[...] = factor
    delta = sums[:, MEM : MEM + 1] - mm_nt(sums[:, 0:MEM], factor, HIGHEST)
    surf[1, c] = (surf[0, c].reshape(CL * CL, MEM) + delta).reshape(CL, CL, MEM)

    swap_of(1).start()
    gram_out[...], _ = total(1, partial(1, c), swap_of(1))

    for bi in range(2):
        swap_of(bi).wait_send()
        copy(got1.at[bi], got1.at[bi], bi, 1, other).wait_send()
        seven = got2.at[bi, pl.ds(0, NZ - 1)]
        copy(seven, seven, bi, 2, other).wait_send()
        copy(got1.at[bi], got1.at[bi], bi, 3, other).wait_send()
        copy(observed.at[bi, blocks], observed.at[bi, blocks], bi, 4, other).wait_send()
        copy(gram.at[bi, c], gram.at[bi, c], bi, 5, other).wait_send()


def in_hbm(*arrays):
    return [pltpu.with_memory_space_constraint(a, pltpu.HBM) for a in arrays]


def observe(ens, st, fr, value, variance):
    batches = st.shape[0]
    outs = (
        (ens.shape, F32),
        ((batches, 2 * MEM + META, NOBS), BF16),
        ((batches, NB, BLK), F32),
        ((BLK, NOBS), BF16),
        ((CL, CL, BLK), F32),
        ((MEM, MEM + 8), F32),
        ((MEM, MEM), F32),
    )
    return pl.pallas_call(
        observe_kernel,
        out_shape=tuple(jax.ShapeDtypeStruct(*o) for o in outs),
        in_specs=[pl.BlockSpec(memory_space=pltpu.HBM)] * 5,
        out_specs=tuple(pl.BlockSpec(memory_space=pltpu.VMEM) for _ in outs),
        scratch_shapes=[
            pltpu.VMEM(ens.shape, F32),
            pltpu.VMEM(st.shape, jnp.int32),
            pltpu.VMEM(fr.shape, F32),
            pltpu.VMEM(value.shape, F32),
            pltpu.VMEM(variance.shape, F32),
            pltpu.VMEM((batches, NC, CL, CL, MEM), F32),
            pltpu.VMEM((batches, HB, MEM, BLK), F32),
            pltpu.VMEM((batches, NX * NY - 1, HB, ROWS, BLK), F32),
            pltpu.VMEM((batches, NZ, HB, ROWS, BLK), F32),
            pltpu.VMEM((batches, NB, MEM, BLK), F32),
            pltpu.VMEM((MEM + 8, NOBS), F32),
            pltpu.VMEM((CL * CL, NOBS), F32),
            pltpu.VMEM((BLK, NOBS), BF16),
            pltpu.VMEM((CL, CL, BLK), F32),
            pltpu.VMEM((2 * MEM, 2 * BLK), BF16),
            pltpu.VMEM((2 * BLK, 2 * MEM), BF16),
            pltpu.VMEM((NC, 2, CL * CL, HB * BLK), BF16),
            pltpu.VMEM((batches, NC, MEM, MEM + 8), F32),
            pltpu.SemaphoreType.DMA((6,)),
            pltpu.SemaphoreType.DMA((batches, 6)),
            pltpu.SemaphoreType.DMA((batches, 6)),
        ],
        compiler_params=pltpu.CompilerParams(
            collective_id=0, has_side_effects=True, vmem_limit_bytes=36 << 20
        ),
        name="observe",
    )(*in_hbm(ens, st, fr, value, variance))


def update_kernel(
    prior, ens, packed, chosen, pick1, taper1, gram, factor0, out,
    work, factor1, apack, spack, taper, base, staged, sems,
):
    x, y, z, c = place()
    lat0 = ((x * NZ + z) * CL).astype(F32)
    lon0 = ((y * NC + c) * CL).astype(F32)

    m = gram[:, 0:MEM] + eye(MEM - 1.0)
    work[0], work[1], low = inverse_start(m)

    def step(exact, low):
        work[0], work[1], low = inverse_step(work[0], work[1], jnp.full((1, 1), low, F32), exact)
        return low[0, 0]

    low = lax.while_loop(lambda v: v < 0.001, functools.partial(step, True), low[0, 0])
    lax.while_loop(lambda v: v < 0.999, functools.partial(step, False), low)
    factor1[...] = spread_factor(inverse_finish(m, work[0]), gram[:, MEM : MEM + 1])

    def chunks_of(bi):
        return (jnp.max(chosen[bi]).astype(jnp.int32) + BLK) // BLK

    chunks = chunks_of(0), chunks_of(1)
    short = jnp.maximum(chunks[0], chunks[1]) <= 1

    def rest(bi, start, factor):
        def one(chunk, carry):
            a, s, lines = gather(packed[bi], one_hot(chosen[bi], chunk), factor[...])
            apack[...] = a
            spack[...] = s
            lon_diff = lon_distance(lon0, join(lines, 3))
            weight = join(lines, 6) / (MEM - 1.0)
            for i in range(CL):
                taper[i] = lat_taper(lat0 + i, join(lines, 0), lon_diff, weight)

            def rows_of(step, carry):
                lats = pl.ds(step * TL, TL)
                staged[lats] += increment(base[lats], apack[...], spack[...], taper[lats])
                return carry

            lax.fori_loop(0, CL // TL, rows_of, 0)
            return carry

        lax.fori_loop(start, chunks[bi], one, 0)

    @pl.when(short)
    def _():
        a, s, _ = gather(packed[1], pick1[...], factor1[...])
        apack[...] = a
        spack[...] = s
        writes = []
        for i in range(CL // TL):
            lats = slice(i * TL, (i + 1) * TL)
            old = ens[lats]
            staged[lats] = old + increment(old, apack[...], spack[...], taper1[lats])
            writes.append(pltpu.make_async_copy(staged.at[lats], out.at[lats], sems.at[i]))
            writes[-1].start()
        for one in writes:
            one.wait()

    @pl.when(jnp.logical_not(short))
    def _():
        pltpu.sync_copy(prior, base)
        staged[...] = ens[...]
        rest(0, 1, factor0)
        base[...] = staged[...]
        rest(1, 0, factor1)
        pltpu.sync_copy(staged, out)


def update(prior, ens, packed, chosen, pick1, taper1, gram, factor0):
    vmem = pl.BlockSpec(memory_space=pltpu.VMEM)
    hbm = pl.BlockSpec(memory_space=pltpu.HBM)
    return pl.pallas_call(
        update_kernel,
        out_shape=jax.ShapeDtypeStruct(prior.shape, F32),
        in_specs=[hbm] + [vmem] * 7,
        out_specs=hbm,
        scratch_shapes=[
            pltpu.VMEM((2, MEM, MEM), F32),
            pltpu.VMEM((MEM, MEM), F32),
            pltpu.VMEM((2 * MEM, 2 * BLK), BF16),
            pltpu.VMEM((2 * BLK, 2 * MEM), BF16),
            pltpu.VMEM((CL, CL, BLK), F32),
            pltpu.VMEM(prior.shape, F32),
            pltpu.VMEM(prior.shape, F32),
            pltpu.SemaphoreType.DMA((CL // TL,)),
        ],
        compiler_params=pltpu.CompilerParams(vmem_limit_bytes=40 << 20),
        name="update",
    )(*in_hbm(prior), ens, packed, chosen, pick1, taper1, gram, factor0)


def local(prior, stencil_rows, obs_frac, obs_value, obs_var):
    st = jnp.transpose(stencil_rows, (0, 2, 1))
    fr = jnp.transpose(obs_frac, (0, 2, 1))
    return update(prior, *observe(prior, st, fr, obs_value, obs_var))


def solution(mesh):
    placed = (P("lat", "lon", None, None), P(), P(), P(), P())
    return jax.shard_map(
        local, mesh=mesh, in_specs=placed, out_specs=P("lat", "lon", None, None), check_vma=False
    )
```

```python
import functools

import jax
import jax.numpy as jnp
from jax import lax
from jax.experimental import pallas as pl
from jax.experimental.pallas import tpu as pltpu
from jax.sharding import PartitionSpec as P

MESH = pl.DeviceIdType.MESH
F32, BF16 = jnp.float32, jnp.bfloat16
HIGHEST = lax.Precision.HIGHEST
NX, NY, NZ, NC = 4, 4, 8, 2
CL = 16
DEPTH = 16
MEM = 128
NOBS = 1024
NLON = 128
BLK = 128
NB = NOBS // BLK
HB = NB // NC
NCH = 2
BC = HB // NCH
ROWS = 8
TL = 4
EXACT, PACKED = 2, 9
META = 16


def split(v):
    hi = v.astype(BF16)
    return hi, (v - hi.astype(F32)).astype(BF16)


def split3(v):
    hi = v.astype(BF16)
    rest = v - hi.astype(F32)
    mid = rest.astype(BF16)
    return hi, mid, (rest - mid.astype(F32)).astype(BF16)


def mm(a, b):
    return jnp.dot(a, b, preferred_element_type=F32)


def mm_nt(a, b, precision=None):
    return lax.dot_general(
        a, b, (((1,), (1,)), ((), ())), preferred_element_type=F32, precision=precision
    )


def place():
    lat, lon = lax.axis_index("lat"), lax.axis_index("lon")
    return lat // NZ, lon // NC, lat % NZ, lon % NC


def hops(step, size):
    return min(step, size - step)


def device(x, y, z, c):
    return (x * NZ + z, y * NC + c)


def eye(scale):
    diagonal = lax.broadcasted_iota(jnp.int32, (MEM, MEM), 0) == lax.broadcasted_iota(
        jnp.int32, (MEM, MEM), 1
    )
    return jnp.where(diagonal, scale, 0.0)


def dot(a, b):
    return jnp.dot(a, b, preferred_element_type=F32, precision=HIGHEST)


def inverse_start(m):
    bound = jnp.max(jnp.sum(jnp.abs(m), axis=0, keepdims=True), axis=1, keepdims=True)
    scale = 1.0 / bound
    return eye(1.0) * scale, m * scale, (MEM - 1.0) * scale


def pack_left(v):
    return jnp.concatenate(split(v), axis=1)


def pack_right(v):
    both = jnp.concatenate(split(v), axis=1)
    return jnp.concatenate([both, both], axis=0)


def packed_dot(left, right):
    both = mm(left, right)
    n = both.shape[1] // 2
    return both[:, 0:n] + both[:, n:]


def inverse_step(x, y, low, exact):
    s = jnp.minimum(2.0 / (1.0 + low), 1.95)
    z = eye(2.0) * s - y * (s * s)
    t = s * low
    low = jnp.minimum(t * (2.0 - t), s * (2.0 - s))
    if exact:
        return dot(x, z), dot(y, z), low
    right = pack_right(z)
    return packed_dot(pack_left(x), right), packed_dot(pack_left(y), right), low


def inverse_finish(m, x):
    return x + dot(x, eye(1.0) - dot(m, x))


def taper_gc(scaled):
    inner_part = (
        ((-0.25 * scaled + 0.5) * scaled + 0.625) * scaled - 5.0 / 3.0
    ) * scaled * scaled + 1.0
    outer_part = (
        ((((scaled / 12.0 - 0.5) * scaled + 0.625) * scaled + 5.0 / 3.0) * scaled - 5.0) * scaled
        + 4.0
        - 2.0 / (3.0 * jnp.maximum(scaled, 1.0))
    )
    return jnp.where(scaled <= 1.0, inner_part, jnp.where(scaled <= 2.0, outer_part, 0.0))


def positions(st, fr, bi, lanes):
    first = st[bi, 0:1, lanes]
    obs_lat = lax.shift_right_logical(first, 11).astype(F32) + fr[bi, 0:1, lanes]
    obs_lon = (lax.shift_right_logical(first, 4) & (NLON - 1)).astype(F32) + fr[bi, 1:2, lanes]
    return obs_lat, obs_lon


def meta_lines(st, fr, variance, bi, lanes, width, innovation):
    obs_lat, obs_lon = positions(st, fr, bi, lanes)
    weight = 1.0 / variance[bi : bi + 1, lanes]
    lines = [*split3(obs_lat), *split3(obs_lon), *split3(weight), *split3(innovation)]
    zero = jnp.zeros((META - len(lines), width), BF16)
    return jnp.concatenate(lines + [zero], axis=0)


def join(got, row):
    return got[row : row + 1] + (got[row + 1 : row + 2] + got[row + 2 : row + 3])


def lon_distance(lon0, obs_lon):
    lon = lax.broadcasted_iota(jnp.int32, (CL, BLK), 0).astype(F32) + lon0
    lon_diff = jnp.abs(lon - obs_lon)
    lon_diff = jnp.minimum(lon_diff, NLON - lon_diff)
    return lon_diff * lon_diff


def lat_taper(lat, obs_lat, lon_diff, weight):
    lat_diff = lat - obs_lat
    return taper_gc(jnp.sqrt(lat_diff * lat_diff + lon_diff) / CL) * weight


def spread_factor(inv, g):
    return (0.5 * (MEM - 1.0)) * inv + jnp.sum(inv * g, axis=0, keepdims=True)


def one_hot(chosen, chunk):
    slot = (lax.broadcasted_iota(jnp.int32, (BLK, BLK), 0) + chunk * BLK).astype(F32)
    return jnp.concatenate(
        [jnp.where(chosen[k : k + 1, :] == slot, 1.0, 0.0).astype(BF16) for k in range(NB)],
        axis=1,
    )


def gather(packed, pick, factor):
    got = mm_nt(packed, pick)
    near_anom = got[0:MEM] + got[MEM : 2 * MEM]
    lines = got[2 * MEM :]
    near_spread = (join(lines, 9) - dot(factor, near_anom)).T
    return pack_right(near_anom), pack_right(near_spread), lines


def increment(state, apack, spack, taper):
    rows = state.shape[0] * CL * DEPTH
    anomaly = state - jnp.mean(state, axis=-1, keepdims=True)
    cov = packed_dot(pack_left(anomaly.reshape(rows, MEM)), apack)
    cov = cov.reshape(state.shape[0], CL, DEPTH, BLK) * taper[:, :, None, :]
    return packed_dot(pack_left(cov.reshape(rows, BLK)), spack).reshape(state.shape)


def observe_kernel(
    ens_in, st_in, fr_in, value_in, var_in,
    ens, packed, chosen, pick1, taper1, gram_out, factor_out,
    state, st, fr, value, variance, surf, part, got1, got2, observed, anom, taper, pick0, taper0,
    apack, spack, wts, gram, load, send, recv,
):
    x, y, z, c = place()
    q = x * NY + y
    lat0 = ((x * NZ + z) * CL).astype(F32)
    lon0 = ((y * NC + c) * CL).astype(F32)
    plane = []
    far = sorted(range(1, NX * NY), key=lambda r: -hops(r // NY, NX) - hops(r % NY, NY))
    for r in far:
        px, py = lax.rem(x + r // NY, NX), lax.rem(y + r % NY, NY)
        plane.append((px * NY + py, device(px, py, z, c)))
    far = sorted(range(1, NZ), key=lambda r: -hops(r, NZ))
    line = [device(x, y, lax.rem(z + r, NZ), c) for r in far]
    other = device(x, y, z, 1 - c)

    def copy(src, dst, bi, stage, target):
        return pltpu.make_async_remote_copy(
            src_ref=src,
            dst_ref=dst,
            send_sem=send.at[bi, stage],
            recv_sem=recv.at[bi, stage],
            device_id=target,
            device_id_type=MESH,
        )

    barrier = pltpu.get_barrier_semaphore()
    partners = line + [d for _, d in plane] + [other]
    for target in partners:
        pl.semaphore_signal(barrier, inc=1, device_id=target, device_id_type=MESH)
    loads = [
        pltpu.make_async_copy(ens_in.at[:, :, 0, :], surf.at[0, c], load.at[0]),
        pltpu.make_async_copy(st_in, st, load.at[1]),
        pltpu.make_async_copy(fr_in, fr, load.at[2]),
        pltpu.make_async_copy(value_in, value, load.at[3]),
        pltpu.make_async_copy(var_in, variance, load.at[4]),
    ]
    load_state = pltpu.make_async_copy(ens_in, state, load.at[5])
    for one in loads:
        one.start()
    for one in loads:
        one.wait()
    load_state.start()

    def span_of(core):
        return pl.ds(pl.multiple_of(core * (HB * BLK), BLK), HB * BLK)

    cells = lax.broadcasted_iota(jnp.int32, (CL, BC * BLK), 0)
    members = pl.ds(pl.multiple_of(q * ROWS, ROWS), ROWS)

    def blocks_of(core, ch):
        return pl.ds(core * HB + ch * BC, BC)

    def lanes_of(core, ch):
        return pl.ds(pl.multiple_of((core * HB + ch * BC) * BLK, BLK), BC * BLK)

    def weights(bi, core, ch):
        span = lanes_of(c, ch)
        first = st[bi, 0:1, span]
        base_lat = lax.shift_right_logical(first, 11)
        base_lon = lax.shift_right_logical(first, 4) & (NLON - 1)
        east = (base_lon + 1) & (NLON - 1)
        fa, fo = fr[bi, 0:1, span], fr[bi, 1:2, span]
        lat = cells + (x * NZ + z) * CL
        lon = cells + (y * NC + core) * CL
        w_lat = jnp.where(lat == base_lat, 1.0 - fa, jnp.where(lat == base_lat + 1, fa, 0.0))
        w_lon = jnp.where(lon == base_lon, 1.0 - fo, jnp.where(lon == east, fo, 0.0))
        return split((w_lat[:, None, :] * w_lon[None, :, :]).reshape(CL * CL, BC * BLK))

    def members_by_cells(bi, core):
        return split(surf[bi, core].reshape(CL * CL, MEM).T)

    def partial(bi, core, ch, parts):
        s_hi, s_lo = parts
        w_hi, w_lo = weights(bi, core, ch) if bi == 0 else (wts[core, ch, 0], wts[core, ch, 1])
        return mm(s_hi, w_hi) + (mm(s_lo, w_hi) + mm(s_hi, w_lo))

    def own_partial(bi):
        parts = members_by_cells(bi, c)
        return [partial(bi, c, ch, parts) for ch in range(NCH)]

    def tapers():
        for k in range(NB):
            lanes = slice(k * BLK, (k + 1) * BLK)
            obs_lat, obs_lon = positions(st, fr, 0, lanes)
            weight = 1.0 / (variance[0:1, lanes] * (MEM - 1.0))
            lon_diff = lon_distance(lon0, obs_lon)

            def one(i, carry):
                rows = pl.ds(pl.multiple_of(i * CL, CL), CL)
                lat = lat0 + lax.convert_element_type(i, F32)
                taper[rows, lanes] = lat_taper(lat, obs_lat, lon_diff, weight)
                return carry

            lax.fori_loop(0, CL, one, 0)

    def select(bi, pick, near_taper):
        obs_lat, obs_lon = positions(st, fr, bi, slice(0, NOBS))
        half = 0.5 * (CL - 1)
        d_lat = jnp.maximum(jnp.abs(obs_lat - (lat0 + half)) - half, 0.0)
        d_lon = jnp.abs(obs_lon - (lon0 + half))
        d_lon = jnp.maximum(jnp.minimum(d_lon, NLON - d_lon) - half, 0.0)
        reach = 2.0 * CL
        near = jnp.where(d_lat * d_lat + d_lon * d_lon <= reach * reach + 0.5, 1.0, 0.0)
        rows = jnp.concatenate([near[:, k * BLK : (k + 1) * BLK] for k in range(NB)], axis=0)
        before = lax.broadcasted_iota(jnp.int32, (BLK, BLK), 0) < lax.broadcasted_iota(
            jnp.int32, (BLK, BLK), 1
        )
        rank = mm(rows.astype(BF16), jnp.where(before, 1.0, 0.0).astype(BF16))
        count = mm(rows.astype(BF16), jnp.ones((BLK, BLK), BF16))
        offset = jnp.zeros((1, BLK), F32)
        for k in range(NB):
            chosen[bi, k : k + 1, :] = jnp.where(
                rows[k : k + 1, :] > 0.0, rank[k : k + 1, :] + offset, -1.0
            )
            offset = offset + count[k : k + 1, :]
        pick[...] = one_hot(chosen[bi], 0)
        lines = meta_lines(st, fr, variance, bi, slice(0, NOBS), NOBS, jnp.zeros((1, NOBS), F32))
        got = mm_nt(lines, pick[...])
        lon_diff = lon_distance(lon0, join(got, 3))
        weight = join(got, 6) / (MEM - 1.0)
        for i in range(CL):
            near_taper[i] = lat_taper(lat0 + i, join(got, 0), lon_diff, weight)

    def update_all():
        load_state.wait()
        a, s, _ = gather(packed[0], pick0[...], factor_out[...])
        apack[...] = a
        spack[...] = s

        def rows_of(step, carry):
            lats = pl.ds(step * TL, TL)
            old = state[lats]
            ens[lats] = old + increment(old, apack[...], spack[...], taper0[lats])
            return carry

        lax.fori_loop(0, CL // TL, rows_of, 0)

    def centre(bi, core, ch):
        for k in range(ch * BC, (ch + 1) * BC):
            lanes = pl.ds(pl.multiple_of((core * HB + k) * BLK, BLK), BLK)
            block = observed[bi, core * HB + k]
            mean = jnp.sum(block, axis=0, keepdims=True) / MEM
            block = block - mean
            innovation = value[bi : bi + 1, lanes] - mean
            anom[0:MEM, lanes] = block
            anom[MEM : MEM + 8, lanes] = jnp.broadcast_to(innovation, (8, BLK))
            hi, lo = split(block)
            packed[bi, 0:MEM, lanes] = hi
            packed[bi, MEM : 2 * MEM, lanes] = lo
            packed[bi, 2 * MEM :, lanes] = meta_lines(st, fr, variance, bi, lanes, BLK, innovation)

    def surface_sums(core):
        half = span_of(core)
        b_hi, b_lo = packed[0, 0:MEM, half], packed[0, MEM : 2 * MEM, half]
        cov = mm(a_hi, b_hi) + (mm(a_lo, b_hi) + mm(a_hi, b_lo))
        return mm_nt(cov * taper[:, half], anom[:, half], HIGHEST)

    def total(bi, mine, swap):
        swap.wait_recv()
        parts = members_by_cells(bi, 1 - c)
        for ch in range(NCH):
            sums = mine[ch] + partial(bi, 1 - c, ch, parts)
            for k in range(BC):
                part[bi, ch * BC + k] = sums[:, k * BLK : (k + 1) * BLK]
            for r, (pq, target) in enumerate(plane):
                rows = pl.ds(pl.multiple_of(pq * ROWS, ROWS), ROWS)
                src = part.at[bi, pl.ds(ch * BC, BC), rows, :]
                copy(src, got1.at[bi, ch, r], bi, 2 + ch, target).start()
        if bi == 0:
            tapers()
        else:
            update_all()
        for ch in range(NCH):
            got = got1.at[bi, ch]
            copy(got, got, bi, 2 + ch, other).wait_recv()
            sums = part[bi, ch * BC : (ch + 1) * BC, members, :]
            for r in range(len(plane)):
                sums = sums + got1[bi, ch, r]
            got2[bi, ch, z] = sums
            for target in line:
                src = got2.at[bi, ch, z]
                copy(src, src, bi, 2 + NCH + ch, target).start()
        if bi == 0:
            select(0, pick0, taper0)
        for ch in range(NCH):
            seven = got2.at[bi, ch, pl.ds(0, NZ - 1)]
            copy(seven, seven, bi, 2 + NCH + ch, other).wait_recv()
            sums = got2[bi, ch, 0]
            for r in range(1, NZ):
                sums = sums + got2[bi, ch, r]
            observed[bi, blocks_of(c, ch), members, :] = sums
            own = observed.at[bi, blocks_of(c, ch), members, :]
            for _, target in plane:
                copy(own, own, bi, 2 + 2 * NCH + ch, target).start()
        if bi == 0:
            select(1, pick1, taper1)
            for core in range(NC):
                for ch in range(NCH):
                    wts[core, ch, 0], wts[core, ch, 1] = weights(1, core, ch)
        normal = None
        for ch in range(NCH):
            got = got1.at[bi, ch]
            copy(got, got, bi, 2 + 2 * NCH + ch, other).wait_recv()
            rows = observed.at[bi, blocks_of(c, ch)]
            copy(rows, rows, bi, 2 + 3 * NCH + ch, other).start()
            centre(bi, c, ch)
            span = lanes_of(c, ch)
            weight = 1.0 / variance[bi : bi + 1, span]
            piece = mm_nt(anom[0:MEM, span] * weight, anom[:, span], HIGHEST)
            normal = piece if normal is None else normal + piece
        gram[bi, c] = normal
        copy(gram.at[bi, c], gram.at[bi, c], bi, 1, other).start()
        sums = surface_sums(c) if bi == 0 else None
        for ch in range(NCH):
            rows = observed.at[bi, blocks_of(c, ch)]
            copy(rows, rows, bi, 2 + 3 * NCH + ch, other).wait_recv()
            centre(bi, 1 - c, ch)
        copy(gram.at[bi, c], gram.at[bi, c], bi, 1, other).wait_recv()
        if bi == 0:
            sums = sums + surface_sums(1 - c)
        return gram[bi, 0] + gram[bi, 1], sums

    def swap_of(bi):
        return copy(surf.at[bi, c], surf.at[bi, c], bi, 0, other)

    mine = own_partial(0)
    surface = surf[0, c].reshape(CL * CL, MEM)
    a_hi, a_lo = split(surface - jnp.mean(surface, axis=-1, keepdims=True))
    pl.semaphore_wait(barrier, len(partners))
    swap_of(0).start()
    normal, sums = total(0, mine, swap_of(0))

    m = normal[:, 0:MEM] + eye(MEM - 1.0)
    x_now, y_now, low = inverse_start(m)
    for i in range(EXACT + PACKED):
        x_now, y_now, low = inverse_step(x_now, y_now, low, i < EXACT)
    factor = spread_factor(inverse_finish(m, x_now), normal[:, MEM : MEM + 1])
    factor_out[...] = factor
    delta = sums[:, MEM : MEM + 1] - mm_nt(sums[:, 0:MEM], factor, HIGHEST)
    surf[1, c] = (surf[0, c].reshape(CL * CL, MEM) + delta).reshape(CL, CL, MEM)

    swap_of(1).start()
    gram_out[...], _ = total(1, own_partial(1), swap_of(1))

    for bi in range(2):
        swap_of(bi).wait_send()
        copy(gram.at[bi, c], gram.at[bi, c], bi, 1, other).wait_send()
        for ch in range(NCH):
            got = got1.at[bi, ch]
            copy(got, got, bi, 2 + ch, other).wait_send()
            seven = got2.at[bi, ch, pl.ds(0, NZ - 1)]
            copy(seven, seven, bi, 2 + NCH + ch, other).wait_send()
            copy(got, got, bi, 2 + 2 * NCH + ch, other).wait_send()
            rows = observed.at[bi, blocks_of(c, ch)]
            copy(rows, rows, bi, 2 + 3 * NCH + ch, other).wait_send()


def in_hbm(*arrays):
    return [pltpu.with_memory_space_constraint(a, pltpu.HBM) for a in arrays]


def observe(ens, st, fr, value, variance):
    batches = st.shape[0]
    outs = (
        (ens.shape, F32),
        ((batches, 2 * MEM + META, NOBS), BF16),
        ((batches, NB, BLK), F32),
        ((BLK, NOBS), BF16),
        ((CL, CL, BLK), F32),
        ((MEM, MEM + 8), F32),
        ((MEM, MEM), F32),
    )
    return pl.pallas_call(
        observe_kernel,
        out_shape=tuple(jax.ShapeDtypeStruct(*o) for o in outs),
        in_specs=[pl.BlockSpec(memory_space=pltpu.HBM)] * 5,
        out_specs=tuple(pl.BlockSpec(memory_space=pltpu.VMEM) for _ in outs),
        scratch_shapes=[
            pltpu.VMEM(ens.shape, F32),
            pltpu.VMEM(st.shape, jnp.int32),
            pltpu.VMEM(fr.shape, F32),
            pltpu.VMEM(value.shape, F32),
            pltpu.VMEM(variance.shape, F32),
            pltpu.VMEM((batches, NC, CL, CL, MEM), F32),
            pltpu.VMEM((batches, HB, MEM, BLK), F32),
            pltpu.VMEM((batches, NCH, NX * NY - 1, BC, ROWS, BLK), F32),
            pltpu.VMEM((batches, NCH, NZ, BC, ROWS, BLK), F32),
            pltpu.VMEM((batches, NB, MEM, BLK), F32),
            pltpu.VMEM((MEM + 8, NOBS), F32),
            pltpu.VMEM((CL * CL, NOBS), F32),
            pltpu.VMEM((BLK, NOBS), BF16),
            pltpu.VMEM((CL, CL, BLK), F32),
            pltpu.VMEM((2 * MEM, 2 * BLK), BF16),
            pltpu.VMEM((2 * BLK, 2 * MEM), BF16),
            pltpu.VMEM((NC, NCH, 2, CL * CL, BC * BLK), BF16),
            pltpu.VMEM((batches, NC, MEM, MEM + 8), F32),
            pltpu.SemaphoreType.DMA((6,)),
            pltpu.SemaphoreType.DMA((batches, 2 + 4 * NCH)),
            pltpu.SemaphoreType.DMA((batches, 2 + 4 * NCH)),
        ],
        compiler_params=pltpu.CompilerParams(
            collective_id=0, has_side_effects=True, vmem_limit_bytes=36 << 20
        ),
        name="observe",
    )(*in_hbm(ens, st, fr, value, variance))


def update_kernel(
    prior, ens, packed, chosen, pick1, taper1, gram, factor0, out,
    work, factor1, apack, spack, taper, base, staged, sems,
):
    x, y, z, c = place()
    lat0 = ((x * NZ + z) * CL).astype(F32)
    lon0 = ((y * NC + c) * CL).astype(F32)

    m = gram[:, 0:MEM] + eye(MEM - 1.0)
    work[0], work[1], low = inverse_start(m)

    def step(exact, low):
        work[0], work[1], low = inverse_step(work[0], work[1], jnp.full((1, 1), low, F32), exact)
        return low[0, 0]

    low = lax.while_loop(lambda v: v < 0.001, functools.partial(step, True), low[0, 0])
    lax.while_loop(lambda v: v < 0.999, functools.partial(step, False), low)
    factor1[...] = spread_factor(inverse_finish(m, work[0]), gram[:, MEM : MEM + 1])

    def chunks_of(bi):
        return (jnp.max(chosen[bi]).astype(jnp.int32) + BLK) // BLK

    chunks = chunks_of(0), chunks_of(1)
    short = jnp.maximum(chunks[0], chunks[1]) <= 1

    def rest(bi, start, factor):
        def one(chunk, carry):
            a, s, lines = gather(packed[bi], one_hot(chosen[bi], chunk), factor[...])
            apack[...] = a
            spack[...] = s
            lon_diff = lon_distance(lon0, join(lines, 3))
            weight = join(lines, 6) / (MEM - 1.0)
            for i in range(CL):
                taper[i] = lat_taper(lat0 + i, join(lines, 0), lon_diff, weight)

            def rows_of(step, carry):
                lats = pl.ds(step * TL, TL)
                staged[lats] += increment(base[lats], apack[...], spack[...], taper[lats])
                return carry

            lax.fori_loop(0, CL // TL, rows_of, 0)
            return carry

        lax.fori_loop(start, chunks[bi], one, 0)

    @pl.when(short)
    def _():
        a, s, _ = gather(packed[1], pick1[...], factor1[...])
        apack[...] = a
        spack[...] = s
        writes = []
        for i in range(CL // TL):
            lats = slice(i * TL, (i + 1) * TL)
            old = ens[lats]
            staged[lats] = old + increment(old, apack[...], spack[...], taper1[lats])
            writes.append(pltpu.make_async_copy(staged.at[lats], out.at[lats], sems.at[i]))
            writes[-1].start()
        for one in writes:
            one.wait()

    @pl.when(jnp.logical_not(short))
    def _():
        pltpu.sync_copy(prior, base)
        staged[...] = ens[...]
        rest(0, 1, factor0)
        base[...] = staged[...]
        rest(1, 0, factor1)
        pltpu.sync_copy(staged, out)


def update(prior, ens, packed, chosen, pick1, taper1, gram, factor0):
    vmem = pl.BlockSpec(memory_space=pltpu.VMEM)
    hbm = pl.BlockSpec(memory_space=pltpu.HBM)
    return pl.pallas_call(
        update_kernel,
        out_shape=jax.ShapeDtypeStruct(prior.shape, F32),
        in_specs=[hbm] + [vmem] * 7,
        out_specs=hbm,
        scratch_shapes=[
            pltpu.VMEM((2, MEM, MEM), F32),
            pltpu.VMEM((MEM, MEM), F32),
            pltpu.VMEM((2 * MEM, 2 * BLK), BF16),
            pltpu.VMEM((2 * BLK, 2 * MEM), BF16),
            pltpu.VMEM((CL, CL, BLK), F32),
            pltpu.VMEM(prior.shape, F32),
            pltpu.VMEM(prior.shape, F32),
            pltpu.SemaphoreType.DMA((CL // TL,)),
        ],
        compiler_params=pltpu.CompilerParams(vmem_limit_bytes=40 << 20),
        name="update",
    )(*in_hbm(prior), ens, packed, chosen, pick1, taper1, gram, factor0)


def local(prior, stencil_rows, obs_frac, obs_value, obs_var):
    st = jnp.transpose(stencil_rows, (0, 2, 1))
    fr = jnp.transpose(obs_frac, (0, 2, 1))
    return update(prior, *observe(prior, st, fr, obs_value, obs_var))


def solution(mesh):
    placed = (P("lat", "lon", None, None), P(), P(), P(), P())
    return jax.shard_map(
        local, mesh=mesh, in_specs=placed, out_specs=P("lat", "lon", None, None), check_vma=False
    )
```

```python
import functools

import jax
import jax.numpy as jnp
from jax import lax
from jax.experimental import pallas as pl
from jax.experimental.pallas import tpu as pltpu
from jax.sharding import PartitionSpec as P

MESH = pl.DeviceIdType.MESH
F32, BF16 = jnp.float32, jnp.bfloat16
HIGHEST = lax.Precision.HIGHEST
NX, NY, NZ, NC = 4, 4, 8, 2
CL = 16
DEPTH = 16
MEM = 128
NOBS = 1024
NLON = 128
BLK = 128
NB = NOBS // BLK
HB = NB // NC
NCH = 2
BC = HB // NCH
ROWS = 8
TL = 4
EXACT, PACKED = 2, 9
META = 16


def split(v):
    hi = v.astype(BF16)
    return hi, (v - hi.astype(F32)).astype(BF16)


def split3(v):
    hi = v.astype(BF16)
    rest = v - hi.astype(F32)
    mid = rest.astype(BF16)
    return hi, mid, (rest - mid.astype(F32)).astype(BF16)


def mm(a, b):
    return jnp.dot(a, b, preferred_element_type=F32)


def mm_nt(a, b, precision=None):
    return lax.dot_general(
        a, b, (((1,), (1,)), ((), ())), preferred_element_type=F32, precision=precision
    )


def place():
    lat, lon = lax.axis_index("lat"), lax.axis_index("lon")
    return lat // NZ, lon // NC, lat % NZ, lon % NC


def hops(step, size):
    return min(step, size - step)


def device(x, y, z, c):
    return (x * NZ + z, y * NC + c)


def eye(scale):
    diagonal = lax.broadcasted_iota(jnp.int32, (MEM, MEM), 0) == lax.broadcasted_iota(
        jnp.int32, (MEM, MEM), 1
    )
    return jnp.where(diagonal, scale, 0.0)


def dot(a, b):
    return jnp.dot(a, b, preferred_element_type=F32, precision=HIGHEST)


def inverse_start(m):
    bound = jnp.max(jnp.sum(jnp.abs(m), axis=0, keepdims=True), axis=1, keepdims=True)
    scale = 1.0 / bound
    return eye(1.0) * scale, m * scale, (MEM - 1.0) * scale


def pack_left(v):
    return jnp.concatenate(split(v), axis=1)


def pack_right(v):
    both = jnp.concatenate(split(v), axis=1)
    return jnp.concatenate([both, both], axis=0)


def packed_dot(left, right):
    both = mm(left, right)
    n = both.shape[1] // 2
    return both[:, 0:n] + both[:, n:]


def inverse_step(x, y, low, exact):
    s = jnp.minimum(2.0 / (1.0 + low), 1.95)
    z = eye(2.0) * s - y * (s * s)
    t = s * low
    low = jnp.minimum(t * (2.0 - t), s * (2.0 - s))
    if exact:
        return dot(x, z), dot(y, z), low
    right = pack_right(z)
    return packed_dot(pack_left(x), right), packed_dot(pack_left(y), right), low


def inverse_finish(m, x):
    return x + dot(x, eye(1.0) - dot(m, x))


def taper_gc(scaled):
    inner_part = (
        ((-0.25 * scaled + 0.5) * scaled + 0.625) * scaled - 5.0 / 3.0
    ) * scaled * scaled + 1.0
    outer_part = (
        ((((scaled / 12.0 - 0.5) * scaled + 0.625) * scaled + 5.0 / 3.0) * scaled - 5.0) * scaled
        + 4.0
        - 2.0 / (3.0 * jnp.maximum(scaled, 1.0))
    )
    return jnp.where(scaled <= 1.0, inner_part, jnp.where(scaled <= 2.0, outer_part, 0.0))


def positions(st, fr, bi, lanes):
    first = st[bi, 0:1, lanes]
    obs_lat = lax.shift_right_logical(first, 11).astype(F32) + fr[bi, 0:1, lanes]
    obs_lon = (lax.shift_right_logical(first, 4) & (NLON - 1)).astype(F32) + fr[bi, 1:2, lanes]
    return obs_lat, obs_lon


def meta_lines(st, fr, variance, bi, lanes, width, innovation):
    obs_lat, obs_lon = positions(st, fr, bi, lanes)
    weight = 1.0 / variance[bi : bi + 1, lanes]
    lines = [*split3(obs_lat), *split3(obs_lon), *split3(weight), *split3(innovation)]
    zero = jnp.zeros((META - len(lines), width), BF16)
    return jnp.concatenate(lines + [zero], axis=0)


def join(got, row):
    return got[row : row + 1] + (got[row + 1 : row + 2] + got[row + 2 : row + 3])


def lon_distance(lon0, obs_lon):
    lon = lax.broadcasted_iota(jnp.int32, (CL, BLK), 0).astype(F32) + lon0
    lon_diff = jnp.abs(lon - obs_lon)
    lon_diff = jnp.minimum(lon_diff, NLON - lon_diff)
    return lon_diff * lon_diff


def lat_taper(lat, obs_lat, lon_diff, weight):
    lat_diff = lat - obs_lat
    return taper_gc(jnp.sqrt(lat_diff * lat_diff + lon_diff) / CL) * weight


def spread_factor(inv, g):
    return (0.5 * (MEM - 1.0)) * inv + jnp.sum(inv * g, axis=0, keepdims=True)


def one_hot(chosen, chunk):
    slot = (lax.broadcasted_iota(jnp.int32, (BLK, BLK), 0) + chunk * BLK).astype(F32)
    return jnp.concatenate(
        [jnp.where(chosen[k : k + 1, :] == slot, 1.0, 0.0).astype(BF16) for k in range(NB)],
        axis=1,
    )


def near_rows(packed, pick):
    got = mm_nt(packed, pick)
    return got[0:MEM] + got[MEM : 2 * MEM], got[2 * MEM :]


def near_spread(near_anom, lines, factor):
    return pack_right((join(lines, 9) - dot(factor, near_anom)).T)


def anomaly_parts(state):
    anomaly = state - jnp.mean(state, axis=-1, keepdims=True)
    return pack_left(anomaly.reshape(state.shape[0] * CL * DEPTH, MEM))


def tapered(parts, apack, taper):
    cov = packed_dot(parts, apack).reshape(TL, CL, DEPTH, BLK) * taper[:, :, None, :]
    return pack_left(cov.reshape(TL * CL * DEPTH, BLK))


def increment(state, apack, spack, taper):
    cov = tapered(anomaly_parts(state), apack, taper)
    return packed_dot(cov, spack).reshape(state.shape)


def observe_kernel(
    ens_in, st_in, fr_in, value_in, var_in,
    ens, packed, chosen, taper1, parts1, near1, apack1, gram_out, factor_out,
    state, pick1, st, fr, value, variance, surf, part, got1, got2, observed, anom, taper, pick0, taper0,
    apack, spack, wts, gram, load, send, recv,
):
    x, y, z, c = place()
    q = x * NY + y
    lat0 = ((x * NZ + z) * CL).astype(F32)
    lon0 = ((y * NC + c) * CL).astype(F32)
    plane = []
    far = sorted(range(1, NX * NY), key=lambda r: -hops(r // NY, NX) - hops(r % NY, NY))
    for r in far:
        px, py = lax.rem(x + r // NY, NX), lax.rem(y + r % NY, NY)
        plane.append((px * NY + py, device(px, py, z, c)))
    far = sorted(range(1, NZ), key=lambda r: -hops(r, NZ))
    line = [device(x, y, lax.rem(z + r, NZ), c) for r in far]
    other = device(x, y, z, 1 - c)

    def copy(src, dst, bi, stage, target):
        return pltpu.make_async_remote_copy(
            src_ref=src,
            dst_ref=dst,
            send_sem=send.at[bi, stage],
            recv_sem=recv.at[bi, stage],
            device_id=target,
            device_id_type=MESH,
        )

    barrier = pltpu.get_barrier_semaphore()
    partners = line + [d for _, d in plane] + [other]
    for target in partners:
        pl.semaphore_signal(barrier, inc=1, device_id=target, device_id_type=MESH)
    loads = [
        pltpu.make_async_copy(st_in, st, load.at[0]),
        pltpu.make_async_copy(fr_in, fr, load.at[1]),
        pltpu.make_async_copy(ens_in.at[:, :, 0, :], surf.at[0, c], load.at[2]),
        pltpu.make_async_copy(value_in, value, load.at[3]),
        pltpu.make_async_copy(var_in, variance, load.at[4]),
    ]
    load_state = pltpu.make_async_copy(ens_in, state, load.at[5])
    for one in loads:
        one.start()
    for one in loads[:2]:
        one.wait()

    def span_of(core):
        return pl.ds(pl.multiple_of(core * (HB * BLK), BLK), HB * BLK)

    cells = lax.broadcasted_iota(jnp.int32, (CL, BC * BLK), 0)
    members = pl.ds(pl.multiple_of(q * ROWS, ROWS), ROWS)

    def blocks_of(core, ch):
        return pl.ds(core * HB + ch * BC, BC)

    def lanes_of(core, ch):
        return pl.ds(pl.multiple_of((core * HB + ch * BC) * BLK, BLK), BC * BLK)

    def weights(bi, core, ch):
        span = lanes_of(c, ch)
        first = st[bi, 0:1, span]
        base_lat = lax.shift_right_logical(first, 11)
        base_lon = lax.shift_right_logical(first, 4) & (NLON - 1)
        east = (base_lon + 1) & (NLON - 1)
        fa, fo = fr[bi, 0:1, span], fr[bi, 1:2, span]
        lat = cells + (x * NZ + z) * CL
        lon = cells + (y * NC + core) * CL
        w_lat = jnp.where(lat == base_lat, 1.0 - fa, jnp.where(lat == base_lat + 1, fa, 0.0))
        w_lon = jnp.where(lon == base_lon, 1.0 - fo, jnp.where(lon == east, fo, 0.0))
        return split((w_lat[:, None, :] * w_lon[None, :, :]).reshape(CL * CL, BC * BLK))

    def members_by_cells(bi, core):
        return split(surf[bi, core].reshape(CL * CL, MEM).T)

    def partial(bi, core, ch, parts):
        s_hi, s_lo = parts
        w_hi, w_lo = weights(bi, core, ch) if bi == 0 else (wts[core, ch, 0], wts[core, ch, 1])
        return mm(s_hi, w_hi) + (mm(s_lo, w_hi) + mm(s_hi, w_lo))

    def own_partial(bi):
        parts = members_by_cells(bi, c)
        return [partial(bi, c, ch, parts) for ch in range(NCH)]

    def tapers():
        for k in range(NB):
            lanes = slice(k * BLK, (k + 1) * BLK)
            obs_lat, obs_lon = positions(st, fr, 0, lanes)
            weight = 1.0 / (variance[0:1, lanes] * (MEM - 1.0))
            lon_diff = lon_distance(lon0, obs_lon)

            def one(i, carry):
                rows = pl.ds(pl.multiple_of(i * CL, CL), CL)
                lat = lat0 + lax.convert_element_type(i, F32)
                taper[rows, lanes] = lat_taper(lat, obs_lat, lon_diff, weight)
                return carry

            lax.fori_loop(0, CL, one, 0)

    def select(bi, pick, near_taper):
        obs_lat, obs_lon = positions(st, fr, bi, slice(0, NOBS))
        half = 0.5 * (CL - 1)
        d_lat = jnp.maximum(jnp.abs(obs_lat - (lat0 + half)) - half, 0.0)
        d_lon = jnp.abs(obs_lon - (lon0 + half))
        d_lon = jnp.maximum(jnp.minimum(d_lon, NLON - d_lon) - half, 0.0)
        reach = 2.0 * CL
        near = jnp.where(d_lat * d_lat + d_lon * d_lon <= reach * reach + 0.5, 1.0, 0.0)
        rows = jnp.concatenate([near[:, k * BLK : (k + 1) * BLK] for k in range(NB)], axis=0)
        before = lax.broadcasted_iota(jnp.int32, (BLK, BLK), 0) < lax.broadcasted_iota(
            jnp.int32, (BLK, BLK), 1
        )
        rank = mm(rows.astype(BF16), jnp.where(before, 1.0, 0.0).astype(BF16))
        count = mm(rows.astype(BF16), jnp.ones((BLK, BLK), BF16))
        offset = jnp.zeros((1, BLK), F32)
        for k in range(NB):
            chosen[bi, k : k + 1, :] = jnp.where(
                rows[k : k + 1, :] > 0.0, rank[k : k + 1, :] + offset, -1.0
            )
            offset = offset + count[k : k + 1, :]
        pick[...] = one_hot(chosen[bi], 0)
        lines = meta_lines(st, fr, variance, bi, slice(0, NOBS), NOBS, jnp.zeros((1, NOBS), F32))
        got = mm_nt(lines, pick[...])
        lon_diff = lon_distance(lon0, join(got, 3))
        weight = join(got, 6) / (MEM - 1.0)
        for i in range(CL):
            near_taper[i] = lat_taper(lat0 + i, join(got, 0), lon_diff, weight)

    def update_all():
        load_state.wait()
        near_anom, lines = near_rows(packed[0], pick0[...])
        apack[...] = pack_right(near_anom)
        spack[...] = near_spread(near_anom, lines, factor_out[...])

        def rows_of(step, carry):
            lats = pl.ds(step * TL, TL)
            old = state[lats]
            new = old + increment(old, apack[...], spack[...], taper0[lats])
            ens[lats] = new
            parts1[step] = anomaly_parts(new)
            return carry

        lax.fori_loop(0, CL // TL, rows_of, 0)

    def centre(bi, core, ch):
        for k in range(ch * BC, (ch + 1) * BC):
            lanes = pl.ds(pl.multiple_of((core * HB + k) * BLK, BLK), BLK)
            block = observed[bi, core * HB + k]
            mean = jnp.sum(block, axis=0, keepdims=True) / MEM
            block = block - mean
            innovation = value[bi : bi + 1, lanes] - mean
            anom[0:MEM, lanes] = block
            anom[MEM : MEM + 8, lanes] = jnp.broadcast_to(innovation, (8, BLK))
            hi, lo = split(block)
            packed[bi, 0:MEM, lanes] = hi
            packed[bi, MEM : 2 * MEM, lanes] = lo
            packed[bi, 2 * MEM :, lanes] = meta_lines(st, fr, variance, bi, lanes, BLK, innovation)

    def surface_sums(core):
        half = span_of(core)
        b_hi, b_lo = packed[0, 0:MEM, half], packed[0, MEM : 2 * MEM, half]
        cov = mm(a_hi, b_hi) + (mm(a_lo, b_hi) + mm(a_hi, b_lo))
        return mm_nt(cov * taper[:, half], anom[:, half], HIGHEST)

    def near_half(core):
        half = span_of(core)
        return mm_nt(packed[1, :, half], pick1[:, half])

    def total(bi, mine, swap):
        swap.wait_recv()
        parts = members_by_cells(bi, 1 - c)
        for ch in range(NCH):
            sums = mine[ch] + partial(bi, 1 - c, ch, parts)
            for k in range(BC):
                part[bi, ch * BC + k] = sums[:, k * BLK : (k + 1) * BLK]
            for r, (pq, target) in enumerate(plane):
                rows = pl.ds(pl.multiple_of(pq * ROWS, ROWS), ROWS)
                src = part.at[bi, pl.ds(ch * BC, BC), rows, :]
                copy(src, got1.at[bi, ch, r], bi, 2 + ch, target).start()
        if bi == 0:
            tapers()
        else:
            update_all()
        for ch in range(NCH):
            got = got1.at[bi, ch]
            copy(got, got, bi, 2 + ch, other).wait_recv()
            sums = part[bi, ch * BC : (ch + 1) * BC, members, :]
            for r in range(len(plane)):
                sums = sums + got1[bi, ch, r]
            got2[bi, ch, z] = sums
            for target in line:
                src = got2.at[bi, ch, z]
                copy(src, src, bi, 2 + NCH + ch, target).start()
        if bi == 0:
            select(0, pick0, taper0)
        for ch in range(NCH):
            seven = got2.at[bi, ch, pl.ds(0, NZ - 1)]
            copy(seven, seven, bi, 2 + NCH + ch, other).wait_recv()
            sums = got2[bi, ch, 0]
            for r in range(1, NZ):
                sums = sums + got2[bi, ch, r]
            observed[bi, blocks_of(c, ch), members, :] = sums
            own = observed.at[bi, blocks_of(c, ch), members, :]
            for _, target in plane:
                copy(own, own, bi, 2 + 2 * NCH + ch, target).start()
        if bi == 0:
            select(1, pick1, taper1)
            for core in range(NC):
                for ch in range(NCH):
                    wts[core, ch, 0], wts[core, ch, 1] = weights(1, core, ch)
        normal = None
        for ch in range(NCH):
            got = got1.at[bi, ch]
            copy(got, got, bi, 2 + 2 * NCH + ch, other).wait_recv()
            rows = observed.at[bi, blocks_of(c, ch)]
            copy(rows, rows, bi, 2 + 3 * NCH + ch, other).start()
            centre(bi, c, ch)
            span = lanes_of(c, ch)
            weight = 1.0 / variance[bi : bi + 1, span]
            piece = mm_nt(anom[0:MEM, span] * weight, anom[:, span], HIGHEST)
            normal = piece if normal is None else normal + piece
        gram[bi, c] = normal
        copy(gram.at[bi, c], gram.at[bi, c], bi, 1, other).start()
        sums = surface_sums(c) if bi == 0 else near_half(c)
        for ch in range(NCH):
            rows = observed.at[bi, blocks_of(c, ch)]
            copy(rows, rows, bi, 2 + 3 * NCH + ch, other).wait_recv()
            centre(bi, 1 - c, ch)
        if bi == 1:
            sums = sums + near_half(1 - c)
            near_anom = sums[0:MEM] + sums[MEM : 2 * MEM]
            near1[0:MEM, :] = near_anom
            near1[MEM:, :] = sums[2 * MEM :]
            apack1[...] = pack_right(near_anom)
        copy(gram.at[bi, c], gram.at[bi, c], bi, 1, other).wait_recv()
        if bi == 0:
            sums = sums + surface_sums(1 - c)
        return gram[bi, 0] + gram[bi, 1], sums

    def swap_of(bi):
        return copy(surf.at[bi, c], surf.at[bi, c], bi, 0, other)

    for one in loads[2:]:
        one.wait()
    load_state.start()
    mine = own_partial(0)
    surface = surf[0, c].reshape(CL * CL, MEM)
    a_hi, a_lo = split(surface - jnp.mean(surface, axis=-1, keepdims=True))
    pl.semaphore_wait(barrier, len(partners))
    swap_of(0).start()
    normal, sums = total(0, mine, swap_of(0))

    m = normal[:, 0:MEM] + eye(MEM - 1.0)
    x_now, y_now, low = inverse_start(m)
    for i in range(EXACT + PACKED):
        x_now, y_now, low = inverse_step(x_now, y_now, low, i < EXACT)
    factor = spread_factor(inverse_finish(m, x_now), normal[:, MEM : MEM + 1])
    factor_out[...] = factor
    delta = sums[:, MEM : MEM + 1] - mm_nt(sums[:, 0:MEM], factor, HIGHEST)
    surf[1, c] = (surf[0, c].reshape(CL * CL, MEM) + delta).reshape(CL, CL, MEM)

    swap_of(1).start()
    gram_out[...], _ = total(1, own_partial(1), swap_of(1))

    for bi in range(2):
        swap_of(bi).wait_send()
        copy(gram.at[bi, c], gram.at[bi, c], bi, 1, other).wait_send()
        for ch in range(NCH):
            got = got1.at[bi, ch]
            copy(got, got, bi, 2 + ch, other).wait_send()
            seven = got2.at[bi, ch, pl.ds(0, NZ - 1)]
            copy(seven, seven, bi, 2 + NCH + ch, other).wait_send()
            copy(got, got, bi, 2 + 2 * NCH + ch, other).wait_send()
            rows = observed.at[bi, blocks_of(c, ch)]
            copy(rows, rows, bi, 2 + 3 * NCH + ch, other).wait_send()


def in_hbm(*arrays):
    return [pltpu.with_memory_space_constraint(a, pltpu.HBM) for a in arrays]


def observe(ens, st, fr, value, variance):
    batches = st.shape[0]
    outs = (
        (ens.shape, F32),
        ((batches, 2 * MEM + META, NOBS), BF16),
        ((batches, NB, BLK), F32),
        ((CL, CL, BLK), F32),
        ((CL // TL, TL * CL * DEPTH, 2 * MEM), BF16),
        ((MEM + META, BLK), F32),
        ((2 * MEM, 2 * BLK), BF16),
        ((MEM, MEM + 8), F32),
        ((MEM, MEM), F32),
    )
    return pl.pallas_call(
        observe_kernel,
        out_shape=tuple(jax.ShapeDtypeStruct(*o) for o in outs),
        in_specs=[pl.BlockSpec(memory_space=pltpu.HBM)] * 5,
        out_specs=tuple(pl.BlockSpec(memory_space=pltpu.VMEM) for _ in outs),
        scratch_shapes=[
            pltpu.VMEM(ens.shape, F32),
            pltpu.VMEM((BLK, NOBS), BF16),
            pltpu.VMEM(st.shape, jnp.int32),
            pltpu.VMEM(fr.shape, F32),
            pltpu.VMEM(value.shape, F32),
            pltpu.VMEM(variance.shape, F32),
            pltpu.VMEM((batches, NC, CL, CL, MEM), F32),
            pltpu.VMEM((batches, HB, MEM, BLK), F32),
            pltpu.VMEM((batches, NCH, NX * NY - 1, BC, ROWS, BLK), F32),
            pltpu.VMEM((batches, NCH, NZ, BC, ROWS, BLK), F32),
            pltpu.VMEM((batches, NB, MEM, BLK), F32),
            pltpu.VMEM((MEM + 8, NOBS), F32),
            pltpu.VMEM((CL * CL, NOBS), F32),
            pltpu.VMEM((BLK, NOBS), BF16),
            pltpu.VMEM((CL, CL, BLK), F32),
            pltpu.VMEM((2 * MEM, 2 * BLK), BF16),
            pltpu.VMEM((2 * BLK, 2 * MEM), BF16),
            pltpu.VMEM((NC, NCH, 2, CL * CL, BC * BLK), BF16),
            pltpu.VMEM((batches, NC, MEM, MEM + 8), F32),
            pltpu.SemaphoreType.DMA((6,)),
            pltpu.SemaphoreType.DMA((batches, 2 + 4 * NCH)),
            pltpu.SemaphoreType.DMA((batches, 2 + 4 * NCH)),
        ],
        compiler_params=pltpu.CompilerParams(
            collective_id=0, has_side_effects=True, vmem_limit_bytes=36 << 20
        ),
        name="observe",
    )(*in_hbm(ens, st, fr, value, variance))


def update_kernel(
    prior, ens, packed, chosen, taper1, parts1, near1, apack1, gram, factor0, out,
    work, factor1, apack, spack, cov, taper, base, staged, sems,
):
    x, y, z, c = place()
    lat0 = ((x * NZ + z) * CL).astype(F32)
    lon0 = ((y * NC + c) * CL).astype(F32)
    tiles = CL // TL

    m = gram[:, 0:MEM] + eye(MEM - 1.0)
    x_now, y_now, low = inverse_start(m)

    def covariances(tile):
        cov[tile] = tapered(parts1[tile], apack1[...], taper1[tile * TL : (tile + 1) * TL])

    def step(low):
        work[0], work[1], low = inverse_step(work[0], work[1], jnp.full((1, 1), low, F32), False)
        return low[0, 0]

    for i in range(EXACT + 3):
        x_now, y_now, low = inverse_step(x_now, y_now, low, i < EXACT)
        if i < tiles:
            covariances(i)
    work[0], work[1] = x_now, y_now
    lax.while_loop(lambda low: low < 0.999, step, low[0, 0])
    factor1[...] = spread_factor(inverse_finish(m, work[0]), gram[:, MEM : MEM + 1])

    def chunks_of(bi):
        return (jnp.max(chosen[bi]).astype(jnp.int32) + BLK) // BLK

    chunks = chunks_of(0), chunks_of(1)
    short = jnp.maximum(chunks[0], chunks[1]) <= 1

    def rest(bi, start, factor):
        def one(chunk, carry):
            near_anom, lines = near_rows(packed[bi], one_hot(chosen[bi], chunk))
            apack[...] = pack_right(near_anom)
            spack[...] = near_spread(near_anom, lines, factor[...])
            lon_diff = lon_distance(lon0, join(lines, 3))
            weight = join(lines, 6) / (MEM - 1.0)
            for i in range(CL):
                taper[i] = lat_taper(lat0 + i, join(lines, 0), lon_diff, weight)

            def rows_of(step, carry):
                lats = pl.ds(step * TL, TL)
                staged[lats] += increment(base[lats], apack[...], spack[...], taper[lats])
                return carry

            lax.fori_loop(0, CL // TL, rows_of, 0)
            return carry

        lax.fori_loop(start, chunks[bi], one, 0)

    @pl.when(short)
    def _():
        spack[...] = near_spread(near1[0:MEM, :], near1[MEM:, :], factor1[...])
        writes = []
        for i in range(tiles):
            lats = slice(i * TL, (i + 1) * TL)
            old = ens[lats]
            staged[lats] = old + packed_dot(cov[i], spack[...]).reshape(old.shape)
            writes.append(pltpu.make_async_copy(staged.at[lats], out.at[lats], sems.at[i]))
            writes[-1].start()
        for one in writes:
            one.wait()

    @pl.when(jnp.logical_not(short))
    def _():
        pltpu.sync_copy(prior, base)
        staged[...] = ens[...]
        rest(0, 1, factor0)
        base[...] = staged[...]
        rest(1, 0, factor1)
        pltpu.sync_copy(staged, out)


def update(prior, *summed):
    vmem = pl.BlockSpec(memory_space=pltpu.VMEM)
    hbm = pl.BlockSpec(memory_space=pltpu.HBM)
    return pl.pallas_call(
        update_kernel,
        out_shape=jax.ShapeDtypeStruct(prior.shape, F32),
        in_specs=[hbm] + [vmem] * len(summed),
        out_specs=hbm,
        scratch_shapes=[
            pltpu.VMEM((2, MEM, MEM), F32),
            pltpu.VMEM((MEM, MEM), F32),
            pltpu.VMEM((2 * MEM, 2 * BLK), BF16),
            pltpu.VMEM((2 * BLK, 2 * MEM), BF16),
            pltpu.VMEM((CL // TL, TL * CL * DEPTH, 2 * BLK), BF16),
            pltpu.VMEM((CL, CL, BLK), F32),
            pltpu.VMEM(prior.shape, F32),
            pltpu.VMEM(prior.shape, F32),
            pltpu.SemaphoreType.DMA((CL // TL,)),
        ],
        compiler_params=pltpu.CompilerParams(vmem_limit_bytes=40 << 20),
        name="update",
    )(*in_hbm(prior), *summed)


def local(prior, stencil_rows, obs_frac, obs_value, obs_var):
    st = jnp.transpose(stencil_rows, (0, 2, 1))
    fr = jnp.transpose(obs_frac, (0, 2, 1))
    return update(prior, *observe(prior, st, fr, obs_value, obs_var))


def solution(mesh):
    placed = (P("lat", "lon", None, None), P(), P(), P(), P())
    return jax.shard_map(
        local, mesh=mesh, in_specs=placed, out_specs=P("lat", "lon", None, None), check_vma=False
    )
```

```python
import functools

import jax
import jax.numpy as jnp
from jax import lax
from jax.experimental import pallas as pl
from jax.experimental.pallas import tpu as pltpu
from jax.sharding import PartitionSpec as P

MESH = pl.DeviceIdType.MESH
F32, BF16 = jnp.float32, jnp.bfloat16
HIGHEST = lax.Precision.HIGHEST
NX, NY, NZ, NC = 4, 4, 8, 2
CL = 16
DEPTH = 16
MEM = 128
NOBS = 1024
NLON = 128
BLK = 128
NB = NOBS // BLK
HB = NB // NC
NCH = 2
BC = HB // NCH
ROWS = 8
TL = 4
EXACT, PACKED = 2, 9
META = 16


def split(v):
    hi = v.astype(BF16)
    return hi, (v - hi.astype(F32)).astype(BF16)


def split3(v):
    hi = v.astype(BF16)
    rest = v - hi.astype(F32)
    mid = rest.astype(BF16)
    return hi, mid, (rest - mid.astype(F32)).astype(BF16)


def mm(a, b):
    return jnp.dot(a, b, preferred_element_type=F32)


def mm_nt(a, b, precision=None):
    return lax.dot_general(
        a, b, (((1,), (1,)), ((), ())), preferred_element_type=F32, precision=precision
    )


def place():
    lat, lon = lax.axis_index("lat"), lax.axis_index("lon")
    return lat // NZ, lon // NC, lat % NZ, lon % NC


def hops(step, size):
    return min(step, size - step)


def device(x, y, z, c):
    return (x * NZ + z, y * NC + c)


def eye(scale):
    diagonal = lax.broadcasted_iota(jnp.int32, (MEM, MEM), 0) == lax.broadcasted_iota(
        jnp.int32, (MEM, MEM), 1
    )
    return jnp.where(diagonal, scale, 0.0)


def dot(a, b):
    return jnp.dot(a, b, preferred_element_type=F32, precision=HIGHEST)


def inverse_start(m):
    bound = jnp.max(jnp.sum(jnp.abs(m), axis=0, keepdims=True), axis=1, keepdims=True)
    scale = 1.0 / bound
    return eye(1.0) * scale, m * scale, (MEM - 1.0) * scale


def pack_left(v):
    return jnp.concatenate(split(v), axis=1)


def pack_right(v):
    both = jnp.concatenate(split(v), axis=1)
    return jnp.concatenate([both, both], axis=0)


def packed_dot(left, right):
    both = mm(left, right)
    n = both.shape[1] // 2
    return both[:, 0:n] + both[:, n:]


def inverse_step(x, y, low, exact):
    s = jnp.minimum(2.0 / (1.0 + low), 1.95)
    z = eye(2.0) * s - y * (s * s)
    t = s * low
    low = jnp.minimum(t * (2.0 - t), s * (2.0 - s))
    if exact:
        return dot(x, z), dot(y, z), low
    right = pack_right(z)
    return packed_dot(pack_left(x), right), packed_dot(pack_left(y), right), low


def inverse_finish(m, x):
    return x + dot(x, eye(1.0) - dot(m, x))


def taper_gc(scaled):
    inner_part = (
        ((-0.25 * scaled + 0.5) * scaled + 0.625) * scaled - 5.0 / 3.0
    ) * scaled * scaled + 1.0
    outer_part = (
        ((((scaled / 12.0 - 0.5) * scaled + 0.625) * scaled + 5.0 / 3.0) * scaled - 5.0) * scaled
        + 4.0
        - 2.0 / (3.0 * jnp.maximum(scaled, 1.0))
    )
    return jnp.where(scaled <= 1.0, inner_part, jnp.where(scaled <= 2.0, outer_part, 0.0))


def positions(st, fr, bi, lanes):
    first = st[bi, 0:1, lanes]
    obs_lat = lax.shift_right_logical(first, 11).astype(F32) + fr[bi, 0:1, lanes]
    obs_lon = (lax.shift_right_logical(first, 4) & (NLON - 1)).astype(F32) + fr[bi, 1:2, lanes]
    return obs_lat, obs_lon


def meta_lines(st, fr, variance, bi, lanes, width, innovation):
    obs_lat, obs_lon = positions(st, fr, bi, lanes)
    weight = 1.0 / variance[bi : bi + 1, lanes]
    lines = [*split3(obs_lat), *split3(obs_lon), *split3(weight), *split3(innovation)]
    zero = jnp.zeros((META - len(lines), width), BF16)
    return jnp.concatenate(lines + [zero], axis=0)


def join(got, row):
    return got[row : row + 1] + (got[row + 1 : row + 2] + got[row + 2 : row + 3])


def lon_distance(lon0, obs_lon):
    lon = lax.broadcasted_iota(jnp.int32, (CL, BLK), 0).astype(F32) + lon0
    lon_diff = jnp.abs(lon - obs_lon)
    lon_diff = jnp.minimum(lon_diff, NLON - lon_diff)
    return lon_diff * lon_diff


def lat_taper(lat, obs_lat, lon_diff, weight):
    lat_diff = lat - obs_lat
    return taper_gc(jnp.sqrt(lat_diff * lat_diff + lon_diff) / CL) * weight


def spread_factor(inv, g):
    return (0.5 * (MEM - 1.0)) * inv + jnp.sum(inv * g, axis=0, keepdims=True)


def one_hot(chosen, chunk):
    slot = (lax.broadcasted_iota(jnp.int32, (BLK, BLK), 0) + chunk * BLK).astype(F32)
    return jnp.concatenate(
        [jnp.where(chosen[k : k + 1, :] == slot, 1.0, 0.0).astype(BF16) for k in range(NB)],
        axis=1,
    )


def near_rows(packed, pick):
    got = mm_nt(packed, pick)
    return got[0:MEM] + got[MEM : 2 * MEM], got[2 * MEM :]


def near_spread(near_anom, lines, factor):
    return pack_right((join(lines, 9) - dot(factor, near_anom)).T)


def anomaly_parts(state):
    anomaly = state - jnp.mean(state, axis=-1, keepdims=True)
    return pack_left(anomaly.reshape(state.shape[0] * CL * DEPTH, MEM))


def tapered(parts, apack, taper):
    cov = packed_dot(parts, apack).reshape(TL, CL, DEPTH, BLK) * taper[:, :, None, :]
    return pack_left(cov.reshape(TL * CL * DEPTH, BLK))


def increment(state, apack, spack, taper):
    cov = tapered(anomaly_parts(state), apack, taper)
    return packed_dot(cov, spack).reshape(state.shape)


def observe_kernel(
    ens_in, st_in, fr_in, value_in, var_in,
    ens, packed, chosen, taper1, parts1, near1, apack1, gram_out, factor_out,
    state, pick1, st, fr, value, variance, surf, part, got1, got2, observed, anom, taper, pick0, taper0,
    apack, spack, wts, gram, load, send, recv,
):
    x, y, z, c = place()
    q = x * NY + y
    lat0 = ((x * NZ + z) * CL).astype(F32)
    lon0 = ((y * NC + c) * CL).astype(F32)
    plane = []
    far = sorted(range(1, NX * NY), key=lambda r: -hops(r // NY, NX) - hops(r % NY, NY))
    for r in far:
        px, py = lax.rem(x + r // NY, NX), lax.rem(y + r % NY, NY)
        plane.append((px * NY + py, device(px, py, z, c)))
    far = sorted(range(1, NZ), key=lambda r: -hops(r, NZ))
    line = [device(x, y, lax.rem(z + r, NZ), c) for r in far]
    other = device(x, y, z, 1 - c)

    def copy(src, dst, bi, stage, target):
        return pltpu.make_async_remote_copy(
            src_ref=src,
            dst_ref=dst,
            send_sem=send.at[bi, stage],
            recv_sem=recv.at[bi, stage],
            device_id=target,
            device_id_type=MESH,
        )

    barrier = pltpu.get_barrier_semaphore()
    partners = line + [d for _, d in plane] + [other]
    for target in partners:
        pl.semaphore_signal(barrier, inc=1, device_id=target, device_id_type=MESH)
    loads = [
        pltpu.make_async_copy(st_in, st, load.at[0]),
        pltpu.make_async_copy(fr_in, fr, load.at[1]),
        pltpu.make_async_copy(ens_in.at[:, :, 0, :], surf.at[0, c], load.at[2]),
        pltpu.make_async_copy(value_in, value, load.at[3]),
        pltpu.make_async_copy(var_in, variance, load.at[4]),
    ]
    load_state = pltpu.make_async_copy(ens_in, state, load.at[5])
    for one in loads:
        one.start()
    for one in loads[:2]:
        one.wait()

    def span_of(core):
        return pl.ds(pl.multiple_of(core * (HB * BLK), BLK), HB * BLK)

    cells = lax.broadcasted_iota(jnp.int32, (CL, BC * BLK), 0)
    members = pl.ds(pl.multiple_of(q * ROWS, ROWS), ROWS)

    def blocks_of(core, ch):
        return pl.ds(core * HB + ch * BC, BC)

    def lanes_of(core, ch):
        return pl.ds(pl.multiple_of((core * HB + ch * BC) * BLK, BLK), BC * BLK)

    def weights(bi, core, ch):
        span = lanes_of(c, ch)
        first = st[bi, 0:1, span]
        base_lat = lax.shift_right_logical(first, 11)
        base_lon = lax.shift_right_logical(first, 4) & (NLON - 1)
        east = (base_lon + 1) & (NLON - 1)
        fa, fo = fr[bi, 0:1, span], fr[bi, 1:2, span]
        lat = cells + (x * NZ + z) * CL
        lon = cells + (y * NC + core) * CL
        w_lat = jnp.where(lat == base_lat, 1.0 - fa, jnp.where(lat == base_lat + 1, fa, 0.0))
        w_lon = jnp.where(lon == base_lon, 1.0 - fo, jnp.where(lon == east, fo, 0.0))
        return split((w_lat[:, None, :] * w_lon[None, :, :]).reshape(CL * CL, BC * BLK))

    def members_by_cells(bi, core):
        return split(surf[bi, core].reshape(CL * CL, MEM).T)

    def partial(bi, core, ch, parts):
        s_hi, s_lo = parts
        w_hi, w_lo = weights(bi, core, ch) if bi == 0 else (wts[core, ch, 0], wts[core, ch, 1])
        return mm(s_hi, w_hi) + (mm(s_lo, w_hi) + mm(s_hi, w_lo))

    def own_partial(bi):
        parts = members_by_cells(bi, c)
        return [partial(bi, c, ch, parts) for ch in range(NCH)]

    def tapers():
        for k in range(NB):
            lanes = slice(k * BLK, (k + 1) * BLK)
            obs_lat, obs_lon = positions(st, fr, 0, lanes)
            weight = 1.0 / (variance[0:1, lanes] * (MEM - 1.0))
            lon_diff = lon_distance(lon0, obs_lon)

            def one(i, carry):
                rows = pl.ds(pl.multiple_of(i * CL, CL), CL)
                lat = lat0 + lax.convert_element_type(i, F32)
                taper[rows, lanes] = lat_taper(lat, obs_lat, lon_diff, weight)
                return carry

            lax.fori_loop(0, CL, one, 0)

    def select(bi, pick, near_taper):
        obs_lat, obs_lon = positions(st, fr, bi, slice(0, NOBS))
        half = 0.5 * (CL - 1)
        d_lat = jnp.maximum(jnp.abs(obs_lat - (lat0 + half)) - half, 0.0)
        d_lon = jnp.abs(obs_lon - (lon0 + half))
        d_lon = jnp.maximum(jnp.minimum(d_lon, NLON - d_lon) - half, 0.0)
        reach = 2.0 * CL
        near = jnp.where(d_lat * d_lat + d_lon * d_lon <= reach * reach + 0.5, 1.0, 0.0)
        rows = jnp.concatenate([near[:, k * BLK : (k + 1) * BLK] for k in range(NB)], axis=0)
        before = lax.broadcasted_iota(jnp.int32, (BLK, BLK), 0) < lax.broadcasted_iota(
            jnp.int32, (BLK, BLK), 1
        )
        rank = mm(rows.astype(BF16), jnp.where(before, 1.0, 0.0).astype(BF16))
        count = mm(rows.astype(BF16), jnp.ones((BLK, BLK), BF16))
        offset = jnp.zeros((1, BLK), F32)
        for k in range(NB):
            chosen[bi, k : k + 1, :] = jnp.where(
                rows[k : k + 1, :] > 0.0, rank[k : k + 1, :] + offset, -1.0
            )
            offset = offset + count[k : k + 1, :]
        pick[...] = one_hot(chosen[bi], 0)
        lines = meta_lines(st, fr, variance, bi, slice(0, NOBS), NOBS, jnp.zeros((1, NOBS), F32))
        got = mm_nt(lines, pick[...])
        lon_diff = lon_distance(lon0, join(got, 3))
        weight = join(got, 6) / (MEM - 1.0)
        for i in range(CL):
            near_taper[i] = lat_taper(lat0 + i, join(got, 0), lon_diff, weight)

    def update_all():
        load_state.wait()
        near_anom, lines = near_rows(packed[0], pick0[...])
        apack[...] = pack_right(near_anom)
        spack[...] = near_spread(near_anom, lines, factor_out[...])

        def rows_of(step, carry):
            lats = pl.ds(step * TL, TL)
            old = state[lats]
            new = old + increment(old, apack[...], spack[...], taper0[lats])
            ens[lats] = new
            parts1[step] = anomaly_parts(new)
            return carry

        lax.fori_loop(0, CL // TL, rows_of, 0)

    def centre(bi, core, ch):
        for k in range(ch * BC, (ch + 1) * BC):
            lanes = pl.ds(pl.multiple_of((core * HB + k) * BLK, BLK), BLK)
            block = observed[bi, core * HB + k]
            mean = jnp.sum(block, axis=0, keepdims=True) / MEM
            block = block - mean
            innovation = value[bi : bi + 1, lanes] - mean
            anom[0:MEM, lanes] = block
            anom[MEM : MEM + 8, lanes] = jnp.broadcast_to(innovation, (8, BLK))
            hi, lo = split(block)
            packed[bi, 0:MEM, lanes] = hi
            packed[bi, MEM : 2 * MEM, lanes] = lo
            packed[bi, 2 * MEM :, lanes] = meta_lines(st, fr, variance, bi, lanes, BLK, innovation)

    def surface_sums(core):
        half = span_of(core)
        b_hi, b_lo = packed[0, 0:MEM, half], packed[0, MEM : 2 * MEM, half]
        cov = mm(a_both, jnp.concatenate([b_hi, b_hi], axis=0))
        cov = cov + mm(a_both, jnp.concatenate([b_lo, b_lo], axis=0))
        cov = cov * taper[:, half]
        cov_hi, cov_lo = split(cov)
        parts = packed[0, 0 : 2 * MEM, half]
        both = mm_nt(cov_hi, parts) + mm_nt(cov_lo, parts)
        pull = jnp.sum(cov * anom[MEM : MEM + 1, half], axis=1, keepdims=True)
        return both[:, 0:MEM] + both[:, MEM:], pull

    def near_half(core):
        half = span_of(core)
        return mm_nt(packed[1, :, half], pick1[:, half])

    def total(bi, mine, swap):
        swap.wait_recv()
        parts = members_by_cells(bi, 1 - c)
        for ch in range(NCH):
            sums = mine[ch] + partial(bi, 1 - c, ch, parts)
            for k in range(BC):
                part[bi, ch * BC + k] = sums[:, k * BLK : (k + 1) * BLK]
            for r, (pq, target) in enumerate(plane):
                rows = pl.ds(pl.multiple_of(pq * ROWS, ROWS), ROWS)
                src = part.at[bi, pl.ds(ch * BC, BC), rows, :]
                copy(src, got1.at[bi, ch, r], bi, 2 + ch, target).start()
        if bi == 0:
            tapers()
        else:
            update_all()
        for ch in range(NCH):
            got = got1.at[bi, ch]
            copy(got, got, bi, 2 + ch, other).wait_recv()
            sums = part[bi, ch * BC : (ch + 1) * BC, members, :]
            for r in range(len(plane)):
                sums = sums + got1[bi, ch, r]
            got2[bi, ch, z] = sums
            for target in line:
                src = got2.at[bi, ch, z]
                copy(src, src, bi, 2 + NCH + ch, target).start()
        if bi == 0:
            select(0, pick0, taper0)
        for ch in range(NCH):
            seven = got2.at[bi, ch, pl.ds(0, NZ - 1)]
            copy(seven, seven, bi, 2 + NCH + ch, other).wait_recv()
            sums = got2[bi, ch, 0]
            for r in range(1, NZ):
                sums = sums + got2[bi, ch, r]
            observed[bi, blocks_of(c, ch), members, :] = sums
            own = observed.at[bi, blocks_of(c, ch), members, :]
            for _, target in plane:
                copy(own, own, bi, 2 + 2 * NCH + ch, target).start()
        if bi == 0:
            select(1, pick1, taper1)
            for core in range(NC):
                for ch in range(NCH):
                    wts[core, ch, 0], wts[core, ch, 1] = weights(1, core, ch)
        normal = None
        for ch in range(NCH):
            got = got1.at[bi, ch]
            copy(got, got, bi, 2 + 2 * NCH + ch, other).wait_recv()
            rows = observed.at[bi, blocks_of(c, ch)]
            copy(rows, rows, bi, 2 + 3 * NCH + ch, other).start()
            centre(bi, c, ch)
            span = lanes_of(c, ch)
            weight = 1.0 / variance[bi : bi + 1, span]
            piece = mm_nt(anom[0:MEM, span] * weight, anom[:, span], HIGHEST)
            normal = piece if normal is None else normal + piece
        gram[bi, c] = normal
        copy(gram.at[bi, c], gram.at[bi, c], bi, 1, other).start()
        sums = surface_sums(c) if bi == 0 else near_half(c)
        for ch in range(NCH):
            rows = observed.at[bi, blocks_of(c, ch)]
            copy(rows, rows, bi, 2 + 3 * NCH + ch, other).wait_recv()
            centre(bi, 1 - c, ch)
        if bi == 1:
            sums = sums + near_half(1 - c)
            near_anom = sums[0:MEM] + sums[MEM : 2 * MEM]
            near1[0:MEM, :] = near_anom
            near1[MEM:, :] = sums[2 * MEM :]
            apack1[...] = pack_right(near_anom)
        copy(gram.at[bi, c], gram.at[bi, c], bi, 1, other).wait_recv()
        if bi == 0:
            more = surface_sums(1 - c)
            sums = sums[0] + more[0], sums[1] + more[1]
        return gram[bi, 0] + gram[bi, 1], sums

    def swap_of(bi):
        return copy(surf.at[bi, c], surf.at[bi, c], bi, 0, other)

    for one in loads[2:]:
        one.wait()
    load_state.start()
    mine = own_partial(0)
    surface = surf[0, c].reshape(CL * CL, MEM)
    a_both = pack_left(surface - jnp.mean(surface, axis=-1, keepdims=True))
    pl.semaphore_wait(barrier, len(partners))
    swap_of(0).start()
    normal, sums = total(0, mine, swap_of(0))

    m = normal[:, 0:MEM] + eye(MEM - 1.0)
    x_now, y_now, low = inverse_start(m)
    for i in range(EXACT + PACKED):
        x_now, y_now, low = inverse_step(x_now, y_now, low, i < EXACT)
    factor = spread_factor(inverse_finish(m, x_now), normal[:, MEM : MEM + 1])
    factor_out[...] = factor
    delta = sums[1] - mm_nt(sums[0], factor, HIGHEST)
    surf[1, c] = (surf[0, c].reshape(CL * CL, MEM) + delta).reshape(CL, CL, MEM)

    swap_of(1).start()
    gram_out[...], _ = total(1, own_partial(1), swap_of(1))

    for bi in range(2):
        swap_of(bi).wait_send()
        copy(gram.at[bi, c], gram.at[bi, c], bi, 1, other).wait_send()
        for ch in range(NCH):
            got = got1.at[bi, ch]
            copy(got, got, bi, 2 + ch, other).wait_send()
            seven = got2.at[bi, ch, pl.ds(0, NZ - 1)]
            copy(seven, seven, bi, 2 + NCH + ch, other).wait_send()
            copy(got, got, bi, 2 + 2 * NCH + ch, other).wait_send()
            rows = observed.at[bi, blocks_of(c, ch)]
            copy(rows, rows, bi, 2 + 3 * NCH + ch, other).wait_send()


def in_hbm(*arrays):
    return [pltpu.with_memory_space_constraint(a, pltpu.HBM) for a in arrays]


def observe(ens, st, fr, value, variance):
    batches = st.shape[0]
    outs = (
        (ens.shape, F32),
        ((batches, 2 * MEM + META, NOBS), BF16),
        ((batches, NB, BLK), F32),
        ((CL, CL, BLK), F32),
        ((CL // TL, TL * CL * DEPTH, 2 * MEM), BF16),
        ((MEM + META, BLK), F32),
        ((2 * MEM, 2 * BLK), BF16),
        ((MEM, MEM + 8), F32),
        ((MEM, MEM), F32),
    )
    return pl.pallas_call(
        observe_kernel,
        out_shape=tuple(jax.ShapeDtypeStruct(*o) for o in outs),
        in_specs=[pl.BlockSpec(memory_space=pltpu.HBM)] * 5,
        out_specs=tuple(pl.BlockSpec(memory_space=pltpu.VMEM) for _ in outs),
        scratch_shapes=[
            pltpu.VMEM(ens.shape, F32),
            pltpu.VMEM((BLK, NOBS), BF16),
            pltpu.VMEM(st.shape, jnp.int32),
            pltpu.VMEM(fr.shape, F32),
            pltpu.VMEM(value.shape, F32),
            pltpu.VMEM(variance.shape, F32),
            pltpu.VMEM((batches, NC, CL, CL, MEM), F32),
            pltpu.VMEM((batches, HB, MEM, BLK), F32),
            pltpu.VMEM((batches, NCH, NX * NY - 1, BC, ROWS, BLK), F32),
            pltpu.VMEM((batches, NCH, NZ, BC, ROWS, BLK), F32),
            pltpu.VMEM((batches, NB, MEM, BLK), F32),
            pltpu.VMEM((MEM + 8, NOBS), F32),
            pltpu.VMEM((CL * CL, NOBS), F32),
            pltpu.VMEM((BLK, NOBS), BF16),
            pltpu.VMEM((CL, CL, BLK), F32),
            pltpu.VMEM((2 * MEM, 2 * BLK), BF16),
            pltpu.VMEM((2 * BLK, 2 * MEM), BF16),
            pltpu.VMEM((NC, NCH, 2, CL * CL, BC * BLK), BF16),
            pltpu.VMEM((batches, NC, MEM, MEM + 8), F32),
            pltpu.SemaphoreType.DMA((6,)),
            pltpu.SemaphoreType.DMA((batches, 2 + 4 * NCH)),
            pltpu.SemaphoreType.DMA((batches, 2 + 4 * NCH)),
        ],
        compiler_params=pltpu.CompilerParams(
            collective_id=0, has_side_effects=True, vmem_limit_bytes=36 << 20
        ),
        name="observe",
    )(*in_hbm(ens, st, fr, value, variance))


def update_kernel(
    prior, ens, packed, chosen, taper1, parts1, near1, apack1, gram, factor0, out,
    work, factor1, apack, spack, cov, taper, base, staged, sems,
):
    x, y, z, c = place()
    lat0 = ((x * NZ + z) * CL).astype(F32)
    lon0 = ((y * NC + c) * CL).astype(F32)
    tiles = CL // TL

    m = gram[:, 0:MEM] + eye(MEM - 1.0)
    x_now, y_now, low = inverse_start(m)

    def covariances(tile):
        cov[tile] = tapered(parts1[tile], apack1[...], taper1[tile * TL : (tile + 1) * TL])

    def step(low):
        work[0], work[1], low = inverse_step(work[0], work[1], jnp.full((1, 1), low, F32), False)
        return low[0, 0]

    for i in range(EXACT + 3):
        x_now, y_now, low = inverse_step(x_now, y_now, low, i < EXACT)
        if i < tiles:
            covariances(i)
    work[0], work[1] = x_now, y_now
    lax.while_loop(lambda low: low < 0.999, step, low[0, 0])
    factor1[...] = spread_factor(inverse_finish(m, work[0]), gram[:, MEM : MEM + 1])

    def chunks_of(bi):
        return (jnp.max(chosen[bi]).astype(jnp.int32) + BLK) // BLK

    chunks = chunks_of(0), chunks_of(1)
    short = jnp.maximum(chunks[0], chunks[1]) <= 1

    def rest(bi, start, factor):
        def one(chunk, carry):
            near_anom, lines = near_rows(packed[bi], one_hot(chosen[bi], chunk))
            apack[...] = pack_right(near_anom)
            spack[...] = near_spread(near_anom, lines, factor[...])
            lon_diff = lon_distance(lon0, join(lines, 3))
            weight = join(lines, 6) / (MEM - 1.0)
            for i in range(CL):
                taper[i] = lat_taper(lat0 + i, join(lines, 0), lon_diff, weight)

            def rows_of(step, carry):
                lats = pl.ds(step * TL, TL)
                staged[lats] += increment(base[lats], apack[...], spack[...], taper[lats])
                return carry

            lax.fori_loop(0, CL // TL, rows_of, 0)
            return carry

        lax.fori_loop(start, chunks[bi], one, 0)

    @pl.when(short)
    def _():
        spack[...] = near_spread(near1[0:MEM, :], near1[MEM:, :], factor1[...])
        writes = []
        for i in range(tiles):
            lats = slice(i * TL, (i + 1) * TL)
            old = ens[lats]
            staged[lats] = old + packed_dot(cov[i], spack[...]).reshape(old.shape)
            writes.append(pltpu.make_async_copy(staged.at[lats], out.at[lats], sems.at[i]))
            writes[-1].start()
        for one in writes:
            one.wait()

    @pl.when(jnp.logical_not(short))
    def _():
        pltpu.sync_copy(prior, base)
        staged[...] = ens[...]
        rest(0, 1, factor0)
        base[...] = staged[...]
        rest(1, 0, factor1)
        pltpu.sync_copy(staged, out)


def update(prior, *summed):
    vmem = pl.BlockSpec(memory_space=pltpu.VMEM)
    hbm = pl.BlockSpec(memory_space=pltpu.HBM)
    return pl.pallas_call(
        update_kernel,
        out_shape=jax.ShapeDtypeStruct(prior.shape, F32),
        in_specs=[hbm] + [vmem] * len(summed),
        out_specs=hbm,
        scratch_shapes=[
            pltpu.VMEM((2, MEM, MEM), F32),
            pltpu.VMEM((MEM, MEM), F32),
            pltpu.VMEM((2 * MEM, 2 * BLK), BF16),
            pltpu.VMEM((2 * BLK, 2 * MEM), BF16),
            pltpu.VMEM((CL // TL, TL * CL * DEPTH, 2 * BLK), BF16),
            pltpu.VMEM((CL, CL, BLK), F32),
            pltpu.VMEM(prior.shape, F32),
            pltpu.VMEM(prior.shape, F32),
            pltpu.SemaphoreType.DMA((CL // TL,)),
        ],
        compiler_params=pltpu.CompilerParams(vmem_limit_bytes=40 << 20),
        name="update",
    )(*in_hbm(prior), *summed)


def local(prior, stencil_rows, obs_frac, obs_value, obs_var):
    st = jnp.transpose(stencil_rows, (0, 2, 1))
    fr = jnp.transpose(obs_frac, (0, 2, 1))
    return update(prior, *observe(prior, st, fr, obs_value, obs_var))


def solution(mesh):
    placed = (P("lat", "lon", None, None), P(), P(), P(), P())
    return jax.shard_map(
        local, mesh=mesh, in_specs=placed, out_specs=P("lat", "lon", None, None), check_vma=False
    )
```

```python
import functools

import jax
import jax.numpy as jnp
from jax import lax
from jax.experimental import pallas as pl
from jax.experimental.pallas import tpu as pltpu
from jax.sharding import PartitionSpec as P

MESH = pl.DeviceIdType.MESH
F32, BF16 = jnp.float32, jnp.bfloat16
HIGHEST = lax.Precision.HIGHEST
NX, NY, NZ, NC = 4, 4, 8, 2
CL = 16
DEPTH = 16
MEM = 128
NOBS = 1024
NLON = 128
BLK = 128
NB = NOBS // BLK
HB = NB // NC
NCH = 2
BC = HB // NCH
ROWS = 8
TL = 4
EXACT, PACKED = 2, 9
META = 16


def split(v):
    hi = v.astype(BF16)
    return hi, (v - hi.astype(F32)).astype(BF16)


def split3(v):
    hi = v.astype(BF16)
    rest = v - hi.astype(F32)
    mid = rest.astype(BF16)
    return hi, mid, (rest - mid.astype(F32)).astype(BF16)


def mm(a, b):
    return jnp.dot(a, b, preferred_element_type=F32)


def mm_nt(a, b, precision=None):
    return lax.dot_general(
        a, b, (((1,), (1,)), ((), ())), preferred_element_type=F32, precision=precision
    )


def place():
    lat, lon = lax.axis_index("lat"), lax.axis_index("lon")
    return lat // NZ, lon // NC, lat % NZ, lon % NC


def hops(step, size):
    return min(step, size - step)


def device(x, y, z, c):
    return (x * NZ + z, y * NC + c)


def eye(scale):
    diagonal = lax.broadcasted_iota(jnp.int32, (MEM, MEM), 0) == lax.broadcasted_iota(
        jnp.int32, (MEM, MEM), 1
    )
    return jnp.where(diagonal, scale, 0.0)


def dot(a, b):
    return jnp.dot(a, b, preferred_element_type=F32, precision=HIGHEST)


def inverse_start(m):
    bound = jnp.max(jnp.sum(jnp.abs(m), axis=0, keepdims=True), axis=1, keepdims=True)
    scale = 1.0 / bound
    return eye(1.0) * scale, m * scale, (MEM - 1.0) * scale


def pack_left(v):
    return jnp.concatenate(split(v), axis=1)


def pack_right(v):
    both = jnp.concatenate(split(v), axis=1)
    return jnp.concatenate([both, both], axis=0)


def packed_dot(left, right):
    both = mm(left, right)
    n = both.shape[1] // 2
    return both[:, 0:n] + both[:, n:]


def inverse_step(x, y, low, exact):
    s = jnp.minimum(2.0 / (1.0 + low), 1.95)
    z = eye(2.0) * s - y * (s * s)
    t = s * low
    low = jnp.minimum(t * (2.0 - t), s * (2.0 - s))
    if exact:
        return dot(x, z), dot(y, z), low
    right = pack_right(z)
    return packed_dot(pack_left(x), right), packed_dot(pack_left(y), right), low


def inverse_finish(m, x):
    return x + dot(x, eye(1.0) - dot(m, x))


def taper_gc(scaled):
    inner_part = (
        ((-0.25 * scaled + 0.5) * scaled + 0.625) * scaled - 5.0 / 3.0
    ) * scaled * scaled + 1.0
    outer_part = (
        ((((scaled / 12.0 - 0.5) * scaled + 0.625) * scaled + 5.0 / 3.0) * scaled - 5.0) * scaled
        + 4.0
        - 2.0 / (3.0 * jnp.maximum(scaled, 1.0))
    )
    return jnp.where(scaled <= 1.0, inner_part, jnp.where(scaled <= 2.0, outer_part, 0.0))


def positions(st, fr, bi, lanes):
    first = st[bi, 0:1, lanes]
    obs_lat = lax.shift_right_logical(first, 11).astype(F32) + fr[bi, 0:1, lanes]
    obs_lon = (lax.shift_right_logical(first, 4) & (NLON - 1)).astype(F32) + fr[bi, 1:2, lanes]
    return obs_lat, obs_lon


def meta_lines(st, fr, variance, bi, lanes, width, innovation):
    obs_lat, obs_lon = positions(st, fr, bi, lanes)
    weight = 1.0 / variance[bi : bi + 1, lanes]
    lines = [*split3(obs_lat), *split3(obs_lon), *split3(weight), *split3(innovation)]
    zero = jnp.zeros((META - len(lines), width), BF16)
    return jnp.concatenate(lines + [zero], axis=0)


def join(got, row):
    return got[row : row + 1] + (got[row + 1 : row + 2] + got[row + 2 : row + 3])


def lon_distance(lon0, obs_lon):
    lon = lax.broadcasted_iota(jnp.int32, (CL, BLK), 0).astype(F32) + lon0
    lon_diff = jnp.abs(lon - obs_lon)
    lon_diff = jnp.minimum(lon_diff, NLON - lon_diff)
    return lon_diff * lon_diff


def lat_taper(lat, obs_lat, lon_diff, weight):
    lat_diff = lat - obs_lat
    return taper_gc(jnp.sqrt(lat_diff * lat_diff + lon_diff) / CL) * weight


def spread_factor(inv, g):
    return (0.5 * (MEM - 1.0)) * inv + jnp.sum(inv * g, axis=0, keepdims=True)


def one_hot(chosen, chunk):
    slot = (lax.broadcasted_iota(jnp.int32, (BLK, BLK), 0) + chunk * BLK).astype(F32)
    return jnp.concatenate(
        [jnp.where(chosen[k : k + 1, :] == slot, 1.0, 0.0).astype(BF16) for k in range(NB)],
        axis=1,
    )


def near_rows(packed, pick):
    got = mm_nt(packed, pick)
    return got[0:MEM] + got[MEM : 2 * MEM], got[2 * MEM :]


def near_spread(near_anom, lines, factor):
    return pack_right((join(lines, 9) - dot(factor, near_anom)).T)


def anomaly_parts(state):
    anomaly = state - jnp.mean(state, axis=-1, keepdims=True)
    return pack_left(anomaly.reshape(state.shape[0] * CL * DEPTH, MEM))


def tapered(parts, apack, taper):
    cov = packed_dot(parts, apack).reshape(TL, CL, DEPTH, BLK) * taper[:, :, None, :]
    return pack_left(cov.reshape(TL * CL * DEPTH, BLK))


def increment(state, apack, spack, taper):
    cov = tapered(anomaly_parts(state), apack, taper)
    return packed_dot(cov, spack).reshape(state.shape)


def observe_kernel(
    ens_in, st_in, fr_in, value_in, var_in,
    ens, packed, chosen, taper1, parts1, near1, apack1, gram_out, factor_out,
    state, pick1, st, fr, value, variance, surf, part, got1, got2, observed, anom, taper, pick0, taper0,
    apack, spack, wts, gram, load, send, recv,
):
    x, y, z, c = place()
    q = x * NY + y
    lat0 = ((x * NZ + z) * CL).astype(F32)
    lon0 = ((y * NC + c) * CL).astype(F32)
    plane = []
    far = sorted(range(1, NX * NY), key=lambda r: -hops(r // NY, NX) - hops(r % NY, NY))
    for r in far:
        px, py = lax.rem(x + r // NY, NX), lax.rem(y + r % NY, NY)
        plane.append((px * NY + py, device(px, py, z, c)))
    far = sorted(range(1, NZ), key=lambda r: -hops(r, NZ))
    line = [device(x, y, lax.rem(z + r, NZ), c) for r in far]
    other = device(x, y, z, 1 - c)

    def copy(src, dst, bi, stage, target):
        return pltpu.make_async_remote_copy(
            src_ref=src,
            dst_ref=dst,
            send_sem=send.at[bi, stage],
            recv_sem=recv.at[bi, stage],
            device_id=target,
            device_id_type=MESH,
        )

    barrier = pltpu.get_barrier_semaphore()
    partners = line + [d for _, d in plane] + [other]
    for target in partners:
        pl.semaphore_signal(barrier, inc=1, device_id=target, device_id_type=MESH)
    loads = [
        pltpu.make_async_copy(st_in, st, load.at[0]),
        pltpu.make_async_copy(fr_in, fr, load.at[1]),
        pltpu.make_async_copy(ens_in.at[:, :, 0, :], surf.at[0, c], load.at[2]),
        pltpu.make_async_copy(value_in, value, load.at[3]),
        pltpu.make_async_copy(var_in, variance, load.at[4]),
    ]
    load_state = pltpu.make_async_copy(ens_in, state, load.at[5])
    for one in loads:
        one.start()
    for one in loads[:2]:
        one.wait()

    def span_of(core):
        return pl.ds(pl.multiple_of(core * (HB * BLK), BLK), HB * BLK)

    cells = lax.broadcasted_iota(jnp.int32, (CL, BC * BLK), 0)
    members = pl.ds(pl.multiple_of(q * ROWS, ROWS), ROWS)

    def blocks_of(core, ch):
        return pl.ds(core * HB + ch * BC, BC)

    def lanes_of(core, ch):
        return pl.ds(pl.multiple_of((core * HB + ch * BC) * BLK, BLK), BC * BLK)

    def weights(bi, core, ch):
        span = lanes_of(c, ch)
        first = st[bi, 0:1, span]
        base_lat = lax.shift_right_logical(first, 11)
        base_lon = lax.shift_right_logical(first, 4) & (NLON - 1)
        east = (base_lon + 1) & (NLON - 1)
        fa, fo = fr[bi, 0:1, span], fr[bi, 1:2, span]
        lat = cells + (x * NZ + z) * CL
        lon = cells + (y * NC + core) * CL
        w_lat = jnp.where(lat == base_lat, 1.0 - fa, jnp.where(lat == base_lat + 1, fa, 0.0))
        w_lon = jnp.where(lon == base_lon, 1.0 - fo, jnp.where(lon == east, fo, 0.0))
        return split((w_lat[:, None, :] * w_lon[None, :, :]).reshape(CL * CL, BC * BLK))

    def members_by_cells(bi, core):
        return split(surf[bi, core].reshape(CL * CL, MEM).T)

    def partial(bi, core, ch, parts):
        s_hi, s_lo = parts
        w_hi, w_lo = weights(bi, core, ch) if bi == 0 else (wts[core, ch, 0], wts[core, ch, 1])
        return mm(s_hi, w_hi) + (mm(s_lo, w_hi) + mm(s_hi, w_lo))

    def own_partial(bi):
        parts = members_by_cells(bi, c)
        return [partial(bi, c, ch, parts) for ch in range(NCH)]

    def tapers():
        for k in range(NB):
            lanes = slice(k * BLK, (k + 1) * BLK)
            obs_lat, obs_lon = positions(st, fr, 0, lanes)
            weight = 1.0 / (variance[0:1, lanes] * (MEM - 1.0))
            lon_diff = lon_distance(lon0, obs_lon)

            def one(i, carry):
                rows = pl.ds(pl.multiple_of(i * CL, CL), CL)
                lat = lat0 + lax.convert_element_type(i, F32)
                taper[rows, lanes] = lat_taper(lat, obs_lat, lon_diff, weight)
                return carry

            lax.fori_loop(0, CL, one, 0)

    def select(bi, pick, near_taper):
        obs_lat, obs_lon = positions(st, fr, bi, slice(0, NOBS))
        half = 0.5 * (CL - 1)
        d_lat = jnp.maximum(jnp.abs(obs_lat - (lat0 + half)) - half, 0.0)
        d_lon = jnp.abs(obs_lon - (lon0 + half))
        d_lon = jnp.maximum(jnp.minimum(d_lon, NLON - d_lon) - half, 0.0)
        reach = 2.0 * CL
        near = jnp.where(d_lat * d_lat + d_lon * d_lon <= reach * reach + 0.5, 1.0, 0.0)
        rows = jnp.concatenate([near[:, k * BLK : (k + 1) * BLK] for k in range(NB)], axis=0)
        before = lax.broadcasted_iota(jnp.int32, (BLK, BLK), 0) < lax.broadcasted_iota(
            jnp.int32, (BLK, BLK), 1
        )
        rank = mm(rows.astype(BF16), jnp.where(before, 1.0, 0.0).astype(BF16))
        count = mm(rows.astype(BF16), jnp.ones((BLK, BLK), BF16))
        offset = jnp.zeros((1, BLK), F32)
        for k in range(NB):
            chosen[bi, k : k + 1, :] = jnp.where(
                rows[k : k + 1, :] > 0.0, rank[k : k + 1, :] + offset, -1.0
            )
            offset = offset + count[k : k + 1, :]
        pick[...] = one_hot(chosen[bi], 0)
        lines = meta_lines(st, fr, variance, bi, slice(0, NOBS), NOBS, jnp.zeros((1, NOBS), F32))
        got = mm_nt(lines, pick[...])
        lon_diff = lon_distance(lon0, join(got, 3))
        weight = join(got, 6) / (MEM - 1.0)
        for i in range(CL):
            near_taper[i] = lat_taper(lat0 + i, join(got, 0), lon_diff, weight)

    def update_all():
        load_state.wait()
        near_anom, lines = near_rows(packed[0], pick0[...])
        apack[...] = pack_right(near_anom)
        spack[...] = near_spread(near_anom, lines, factor_out[...])

        def rows_of(step, carry):
            lats = pl.ds(step * TL, TL)
            old = state[lats]
            new = old + increment(old, apack[...], spack[...], taper0[lats])
            ens[lats] = new
            parts1[step] = anomaly_parts(new)
            return carry

        lax.fori_loop(0, CL // TL, rows_of, 0)

    def centre(bi, core, ch):
        for k in range(ch * BC, (ch + 1) * BC):
            lanes = pl.ds(pl.multiple_of((core * HB + k) * BLK, BLK), BLK)
            block = observed[bi, core * HB + k]
            mean = jnp.sum(block, axis=0, keepdims=True) / MEM
            block = block - mean
            innovation = value[bi : bi + 1, lanes] - mean
            anom[0:MEM, lanes] = block
            anom[MEM : MEM + 8, lanes] = jnp.broadcast_to(innovation, (8, BLK))
            hi, lo = split(block)
            packed[bi, 0:MEM, lanes] = hi
            packed[bi, MEM : 2 * MEM, lanes] = lo
            packed[bi, 2 * MEM :, lanes] = meta_lines(st, fr, variance, bi, lanes, BLK, innovation)

    def surface_sums(core):
        half = span_of(core)
        b_hi, b_lo = packed[0, 0:MEM, half], packed[0, MEM : 2 * MEM, half]
        cov = mm(a_hi, b_hi) + (mm(a_lo, b_hi) + mm(a_hi, b_lo))
        return mm_nt(cov * taper[:, half], anom[:, half], HIGHEST)

    def near_half(core):
        half = span_of(core)
        return mm_nt(packed[1, :, half], pick1[:, half])

    def total(bi, mine, swap):
        swap.wait_recv()
        parts = members_by_cells(bi, 1 - c)
        for ch in range(NCH):
            sums = mine[ch] + partial(bi, 1 - c, ch, parts)
            for k in range(BC):
                part[bi, ch * BC + k] = sums[:, k * BLK : (k + 1) * BLK]
            for r, (pq, target) in enumerate(plane):
                rows = pl.ds(pl.multiple_of(pq * ROWS, ROWS), ROWS)
                src = part.at[bi, pl.ds(ch * BC, BC), rows, :]
                copy(src, got1.at[bi, ch, r], bi, 2 + ch, target).start()
        if bi == 0:
            tapers()
        else:
            update_all()
        for ch in range(NCH):
            got = got1.at[bi, ch]
            copy(got, got, bi, 2 + ch, other).wait_recv()
            sums = part[bi, ch * BC : (ch + 1) * BC, members, :]
            for r in range(len(plane)):
                sums = sums + got1[bi, ch, r]
            got2[bi, ch, z] = sums
            for target in line:
                src = got2.at[bi, ch, z]
                copy(src, src, bi, 2 + NCH + ch, target).start()
        if bi == 0:
            select(0, pick0, taper0)
        for ch in range(NCH):
            seven = got2.at[bi, ch, pl.ds(0, NZ - 1)]
            copy(seven, seven, bi, 2 + NCH + ch, other).wait_recv()
            sums = got2[bi, ch, 0]
            for r in range(1, NZ):
                sums = sums + got2[bi, ch, r]
            observed[bi, blocks_of(c, ch), members, :] = sums
            own = observed.at[bi, blocks_of(c, ch), members, :]
            for _, target in plane:
                copy(own, own, bi, 2 + 2 * NCH + ch, target).start()
        if bi == 0:
            select(1, pick1, taper1)
            for core in range(NC):
                for ch in range(NCH):
                    wts[core, ch, 0], wts[core, ch, 1] = weights(1, core, ch)
        normal = None
        for ch in range(NCH):
            got = got1.at[bi, ch]
            copy(got, got, bi, 2 + 2 * NCH + ch, other).wait_recv()
            rows = observed.at[bi, blocks_of(c, ch)]
            copy(rows, rows, bi, 2 + 3 * NCH + ch, other).start()
            centre(bi, c, ch)
            span = lanes_of(c, ch)
            weight = 1.0 / variance[bi : bi + 1, span]
            piece = mm_nt(anom[0:MEM, span] * weight, anom[:, span], HIGHEST)
            normal = piece if normal is None else normal + piece
        gram[bi, c] = normal
        copy(gram.at[bi, c], gram.at[bi, c], bi, 1, other).start()
        sums = surface_sums(c) if bi == 0 else near_half(c)
        for ch in range(NCH):
            rows = observed.at[bi, blocks_of(c, ch)]
            copy(rows, rows, bi, 2 + 3 * NCH + ch, other).wait_recv()
            centre(bi, 1 - c, ch)
        if bi == 1:
            sums = sums + near_half(1 - c)
            near_anom = sums[0:MEM] + sums[MEM : 2 * MEM]
            near1[0:MEM, :] = near_anom
            near1[MEM:, :] = sums[2 * MEM :]
            apack1[...] = pack_right(near_anom)
        copy(gram.at[bi, c], gram.at[bi, c], bi, 1, other).wait_recv()
        if bi == 0:
            sums = sums + surface_sums(1 - c)
        return gram[bi, 0] + gram[bi, 1], sums

    def swap_of(bi):
        return copy(surf.at[bi, c], surf.at[bi, c], bi, 0, other)

    for one in loads[2:]:
        one.wait()
    load_state.start()
    mine = own_partial(0)
    surface = surf[0, c].reshape(CL * CL, MEM)
    a_hi, a_lo = split(surface - jnp.mean(surface, axis=-1, keepdims=True))
    pl.semaphore_wait(barrier, len(partners))
    swap_of(0).start()
    normal, sums = total(0, mine, swap_of(0))

    m = normal[:, 0:MEM] + eye(MEM - 1.0)
    x_now, y_now, low = inverse_start(m)
    for i in range(EXACT + PACKED):
        x_now, y_now, low = inverse_step(x_now, y_now, low, i < EXACT)
    factor = spread_factor(inverse_finish(m, x_now), normal[:, MEM : MEM + 1])
    factor_out[...] = factor
    delta = sums[:, MEM : MEM + 1] - mm_nt(sums[:, 0:MEM], factor, HIGHEST)
    surf[1, c] = (surf[0, c].reshape(CL * CL, MEM) + delta).reshape(CL, CL, MEM)

    swap_of(1).start()
    gram_out[...], _ = total(1, own_partial(1), swap_of(1))

    for bi in range(2):
        swap_of(bi).wait_send()
        copy(gram.at[bi, c], gram.at[bi, c], bi, 1, other).wait_send()
        for ch in range(NCH):
            got = got1.at[bi, ch]
            copy(got, got, bi, 2 + ch, other).wait_send()
            seven = got2.at[bi, ch, pl.ds(0, NZ - 1)]
            copy(seven, seven, bi, 2 + NCH + ch, other).wait_send()
            copy(got, got, bi, 2 + 2 * NCH + ch, other).wait_send()
            rows = observed.at[bi, blocks_of(c, ch)]
            copy(rows, rows, bi, 2 + 3 * NCH + ch, other).wait_send()


def in_hbm(*arrays):
    return [pltpu.with_memory_space_constraint(a, pltpu.HBM) for a in arrays]


def observe(ens, st, fr, value, variance):
    batches = st.shape[0]
    outs = (
        (ens.shape, F32),
        ((batches, 2 * MEM + META, NOBS), BF16),
        ((batches, NB, BLK), F32),
        ((CL, CL, BLK), F32),
        ((CL // TL, TL * CL * DEPTH, 2 * MEM), BF16),
        ((MEM + META, BLK), F32),
        ((2 * MEM, 2 * BLK), BF16),
        ((MEM, MEM + 8), F32),
        ((MEM, MEM), F32),
    )
    return pl.pallas_call(
        observe_kernel,
        out_shape=tuple(jax.ShapeDtypeStruct(*o) for o in outs),
        in_specs=[pl.BlockSpec(memory_space=pltpu.HBM)] * 5,
        out_specs=tuple(pl.BlockSpec(memory_space=pltpu.VMEM) for _ in outs),
        scratch_shapes=[
            pltpu.VMEM(ens.shape, F32),
            pltpu.VMEM((BLK, NOBS), BF16),
            pltpu.VMEM(st.shape, jnp.int32),
            pltpu.VMEM(fr.shape, F32),
            pltpu.VMEM(value.shape, F32),
            pltpu.VMEM(variance.shape, F32),
            pltpu.VMEM((batches, NC, CL, CL, MEM), F32),
            pltpu.VMEM((batches, HB, MEM, BLK), F32),
            pltpu.VMEM((batches, NCH, NX * NY - 1, BC, ROWS, BLK), F32),
            pltpu.VMEM((batches, NCH, NZ, BC, ROWS, BLK), F32),
            pltpu.VMEM((batches, NB, MEM, BLK), F32),
            pltpu.VMEM((MEM + 8, NOBS), F32),
            pltpu.VMEM((CL * CL, NOBS), F32),
            pltpu.VMEM((BLK, NOBS), BF16),
            pltpu.VMEM((CL, CL, BLK), F32),
            pltpu.VMEM((2 * MEM, 2 * BLK), BF16),
            pltpu.VMEM((2 * BLK, 2 * MEM), BF16),
            pltpu.VMEM((NC, NCH, 2, CL * CL, BC * BLK), BF16),
            pltpu.VMEM((batches, NC, MEM, MEM + 8), F32),
            pltpu.SemaphoreType.DMA((6,)),
            pltpu.SemaphoreType.DMA((batches, 2 + 4 * NCH)),
            pltpu.SemaphoreType.DMA((batches, 2 + 4 * NCH)),
        ],
        compiler_params=pltpu.CompilerParams(
            collective_id=0, has_side_effects=True, vmem_limit_bytes=36 << 20
        ),
        name="observe",
    )(*in_hbm(ens, st, fr, value, variance))


def update_kernel(
    prior, ens, packed, chosen, taper1, parts1, near1, apack1, gram, factor0, out,
    work, factor1, apack, spack, cov, taper, base, staged, sems,
):
    x, y, z, c = place()
    lat0 = ((x * NZ + z) * CL).astype(F32)
    lon0 = ((y * NC + c) * CL).astype(F32)
    tiles = CL // TL

    m = gram[:, 0:MEM] + eye(MEM - 1.0)
    x_now, y_now, low = inverse_start(m)

    def covariances(tile):
        cov[tile] = tapered(parts1[tile], apack1[...], taper1[tile * TL : (tile + 1) * TL])

    def step(low):
        work[0], work[1], low = inverse_step(work[0], work[1], jnp.full((1, 1), low, F32), False)
        return low[0, 0]

    for i in range(EXACT + 3):
        x_now, y_now, low = inverse_step(x_now, y_now, low, i < EXACT)
        if i < tiles:
            covariances(i)
    work[0], work[1] = x_now, y_now
    lax.while_loop(lambda low: low < 0.999, step, low[0, 0])
    factor1[...] = spread_factor(inverse_finish(m, work[0]), gram[:, MEM : MEM + 1])

    def chunks_of(bi):
        return (jnp.max(chosen[bi]).astype(jnp.int32) + BLK) // BLK

    chunks = chunks_of(0), chunks_of(1)
    short = jnp.maximum(chunks[0], chunks[1]) <= 1

    def rest(bi, start, factor):
        def one(chunk, carry):
            near_anom, lines = near_rows(packed[bi], one_hot(chosen[bi], chunk))
            apack[...] = pack_right(near_anom)
            spack[...] = near_spread(near_anom, lines, factor[...])
            lon_diff = lon_distance(lon0, join(lines, 3))
            weight = join(lines, 6) / (MEM - 1.0)
            for i in range(CL):
                taper[i] = lat_taper(lat0 + i, join(lines, 0), lon_diff, weight)

            def rows_of(step, carry):
                lats = pl.ds(step * TL, TL)
                staged[lats] += increment(base[lats], apack[...], spack[...], taper[lats])
                return carry

            lax.fori_loop(0, CL // TL, rows_of, 0)
            return carry

        lax.fori_loop(start, chunks[bi], one, 0)

    @pl.when(short)
    def _():
        spack[...] = near_spread(near1[0:MEM, :], near1[MEM:, :], factor1[...])
        writes = []
        part = TL // 2
        for i in range(2 * tiles):
            lats = slice(i * part, (i + 1) * part)
            old = ens[lats]
            rows = slice(i % 2 * part * CL * DEPTH, (i % 2 + 1) * part * CL * DEPTH)
            staged[lats] = old + packed_dot(cov[i // 2, rows, :], spack[...]).reshape(old.shape)
            writes.append(pltpu.make_async_copy(staged.at[lats], out.at[lats], sems.at[i]))
            writes[-1].start()
        for one in writes:
            one.wait()

    @pl.when(jnp.logical_not(short))
    def _():
        pltpu.sync_copy(prior, base)
        staged[...] = ens[...]
        rest(0, 1, factor0)
        base[...] = staged[...]
        rest(1, 0, factor1)
        pltpu.sync_copy(staged, out)


def update(prior, *summed):
    vmem = pl.BlockSpec(memory_space=pltpu.VMEM)
    hbm = pl.BlockSpec(memory_space=pltpu.HBM)
    return pl.pallas_call(
        update_kernel,
        out_shape=jax.ShapeDtypeStruct(prior.shape, F32),
        in_specs=[hbm] + [vmem] * len(summed),
        out_specs=hbm,
        scratch_shapes=[
            pltpu.VMEM((2, MEM, MEM), F32),
            pltpu.VMEM((MEM, MEM), F32),
            pltpu.VMEM((2 * MEM, 2 * BLK), BF16),
            pltpu.VMEM((2 * BLK, 2 * MEM), BF16),
            pltpu.VMEM((CL // TL, TL * CL * DEPTH, 2 * BLK), BF16),
            pltpu.VMEM((CL, CL, BLK), F32),
            pltpu.VMEM(prior.shape, F32),
            pltpu.VMEM(prior.shape, F32),
            pltpu.SemaphoreType.DMA((2 * CL // TL,)),
        ],
        compiler_params=pltpu.CompilerParams(vmem_limit_bytes=40 << 20),
        name="update",
    )(*in_hbm(prior), *summed)


def local(prior, stencil_rows, obs_frac, obs_value, obs_var):
    st = jnp.transpose(stencil_rows, (0, 2, 1))
    fr = jnp.transpose(obs_frac, (0, 2, 1))
    return update(prior, *observe(prior, st, fr, obs_value, obs_var))


def solution(mesh):
    placed = (P("lat", "lon", None, None), P(), P(), P(), P())
    return jax.shard_map(
        local, mesh=mesh, in_specs=placed, out_specs=P("lat", "lon", None, None), check_vma=False
    )
```
